32 devices in a mesh: groups: 2 (over x), section: 8 (over z, y), tensor: 2 (over core).
Axes of the slice: x: 2, y: 2, z: 4, core: 2. Of those that a mesh axis runs over, the one named last changes fastest.
Arguments:
- tokens: bfloat16 [4096, 8192], P(('groups', 'section'), 'tensor'), parts along dimension 0, may hold values from -6 to 6
- norm_gain: bfloat16 [8192], P('tensor'), may hold values from 0.099609375 to 1.8984375
- kv_weight: bfloat16 [8192, 1024], P('tensor'), may hold values from -0.0625 to 0.0625
- lengths: int32 [16, 8], P(('groups', 'section')), parts along dimension 0, may hold values from 1 to 96, 256 in all within a row
- decode_host: int32 [16, 8], P(('groups', 'section')), parts along dimension 0, may hold values from 0 to 7, as said below
- beam_counts: int32 [16, 8], P(('groups', 'section')), parts along dimension 0, may hold values from 4 to 16, as said below
- beam_query: bfloat16 [1280, 4096], P(('groups', 'section'), 'tensor'), parts along dimension 0, may hold values from -200 to 200
- beam_newkv: bfloat16 [1280, 1024], P(('groups', 'section'), 'tensor'), parts along dimension 0, may hold values from -6 to 6
Outputs:
- context: bfloat16 [1280, 4096], P(('groups', 'section'), 'tensor'), parts along dimension 0
The draws below stay inside these ranges and needn't reach their ends.
There are 2 independent parts, one for each index of `groups`. The reference program is written for one: setup_inputs(seed, part) draws one part's arguments, and reference() takes and returns one part's arrays. A program takes and returns all parts, laid end to end along the dimension named above; an argument that names none is the same for every part. Nothing has to cross between parts.
Inputs may be any that keep to these rules, and one draw needn't show every extreme that they name: `lengths`: each row sums to 256; prompt i of a prefill device fills its token rows right after prompts 0 to i - 1. decode_host[s, i] is the decode device along section that holds the beams of prompt i of prefill device s. The 8 prompts of one prefill device go to different decode devices, and every decode device receives, for each i, the prompt i of exactly one prefill device. beam_counts[d, j] is the number of beams on decode device d for the prompt it receives with index j. Each row sums to 80.
All inputs are finite; a program needn't handle non-finite values.
Results may differ from the reference program's by a relative error of at most 0.012.
The reference program's roundings to bfloat16 on the way (of `scaled`, `prompt_kv` and `weights`) count: a program that leaves them out, or rounds other values in their place, can miss the bound.
Values may be sent and summed in bfloat16 or wider, within the bound.
No kernel may reach another device: no remote copies, remote signals or barrier semaphores. Data moves between devices by JAX's collectives and lax.ppermute only.
A program may use at most 128 MiB of HBM per device.

```python
import math
import jax
import jax.numpy as jnp
import numpy as np
from jax import lax

D = 8192
KVH = 4
QPK = 8
HD = 128
BMIN = 4
BMAX = 16
PR_DEV = 8
TOK_DEV = 256
MAXLEN = 96
BEAM_DEV = 80
PROMPT_ROWS = 2048
BEAMS = 640
N_SECTION = 8


def draw_decode_host(key, part):
    key = jax.random.fold_in(key, 11)
    first, second, third = jax.random.split(key, 3)
    source_perm = jax.random.permutation(first, N_SECTION).astype(jnp.int32)
    target_perm = jax.random.permutation(second, N_SECTION).astype(jnp.int32)
    shifts = jax.random.permutation(third, N_SECTION).astype(jnp.int32)[:PR_DEV]
    position = (source_perm[:, None] + shifts[None, :]) % N_SECTION
    return target_perm[position].astype(jnp.int32)


def draw_beam_counts(key, part):
    key = jax.random.fold_in(key, 23)
    first, second = jax.random.split(key)
    center = (BMIN + BMAX) // 2
    spread = (BMAX - BMIN) // 2
    half = PR_DEV // 2
    amounts = jax.random.randint(first, (N_SECTION, half), 0, spread + 1)
    amounts = amounts.at[:, 0].set(spread)
    values = jnp.concatenate([center + amounts, center - amounts], axis=1)
    row_keys = jax.random.split(second, N_SECTION)
    orders = jax.vmap(lambda row_key: jax.random.permutation(row_key, PR_DEV))(row_keys)
    return jnp.take_along_axis(values, orders, axis=1).astype(jnp.int32)


def draw_beam_query(key, part):
    key = jax.random.fold_in(key, 37)
    second = jax.random.fold_in(key, 1)
    values = jnp.clip(jax.random.normal(second, (BEAMS, KVH * QPK * HD), jnp.float32), -6.0, 6.0)
    return values.astype(jnp.bfloat16)


def level_of(own_key, extent, cuts, low, largest):
    factor_of = 1.0
    for axis_at, blocks in cuts:
        draws = jax.random.uniform(jax.random.fold_in(jax.random.fold_in(own_key, 6), axis_at), (blocks,), jnp.float32, low / len(cuts), largest / len(cuts))
        factor_of = factor_of * jnp.repeat(jnp.exp(draws), extent[axis_at] // blocks).reshape((-1,) + (1,) * (len(extent) - 1 - axis_at))
    return factor_of


def profile(number_of, total, limit, slope):
    loads = [(1 << 20) // math.isqrt(standing ** slope) + 1 for standing in range(2, number_of + 1)]
    surplus, given = total - limit - (number_of - 1), [1] * (number_of - 1)
    while surplus > 0:
        free = [i for i in range(number_of - 1) if given[i] < limit]
        mass, budget = sum([loads[i] for i in free]), surplus
        for i in free:
            addition = min(limit - given[i], max(1, budget * loads[i] // mass), surplus)
            given[i] = given[i] + addition
            surplus = surplus - addition
    return np.array([limit] + given)


def ragged_sizes(key, amount, total, most, skew):
    if amount == 2:
        one = jax.random.randint(key, (), max(1, total - most), min(most, total - 1) + 1)
        return jnp.stack([one, total - one])
    tallies = jnp.asarray(profile(amount, total, most, skew), jnp.int32)
    couples = (amount - 1) // 2
    source_of, sink = tallies[1:1 + 2 * couples:2], tallies[2:2 + 2 * couples:2]
    margin = jnp.minimum(source_of - 1, most - sink)
    passed = jax.random.randint(jax.random.fold_in(key, 1), (couples,), 0, 1 << 20) % (margin + 1)
    tallies = tallies.at[1:1 + 2 * couples:2].set(source_of - passed).at[2:2 + 2 * couples:2].set(sink + passed)
    return tallies[jax.random.permutation(jax.random.fold_in(key, 2), amount)]


def noise(own_key, extent, deviation, bound, shards=(), held_as=jnp.bfloat16):
    entries = jax.random.normal(own_key, extent, jnp.float32) * deviation
    if len(shards) > 0:
        entries = level_of(own_key, extent, shards, -0.22, 0.18) * entries
    return jnp.clip(entries, min=-bound, max=bound).astype(held_as)


def setup_inputs(seed: int = 0, part: int = 0) -> dict:
    seeds = jax.random.split(jax.random.key(seed), 9)
    part_splits = jax.random.split(jax.random.fold_in(seeds[8], part), 9)
    return {
        "tokens": noise(part_splits[0], (PROMPT_ROWS, D), 1.0, 6.0, ((0, 8), (1, 2))),
        "norm_gain": jnp.clip(1.0 + 0.18 * jax.random.normal(seeds[1], (D,), jnp.float32), 0.099609375, 1.8984375).astype(jnp.bfloat16),
        "kv_weight": noise(seeds[2], (D, 2 * KVH * HD), D ** -0.5, 0.0625, ((0, 2),)),
        "lengths": jax.vmap(lambda own: ragged_sizes(own, PR_DEV, TOK_DEV, MAXLEN, 2))(jax.random.split(part_splits[3], N_SECTION)).reshape((N_SECTION, PR_DEV)).astype(jnp.int32),
        "decode_host": draw_decode_host(jax.random.fold_in(jax.random.fold_in(seeds[8], part), 71), part),
        "beam_counts": draw_beam_counts(jax.random.fold_in(jax.random.fold_in(seeds[8], part), 71), part),
        "beam_query": draw_beam_query(jax.random.fold_in(jax.random.fold_in(seeds[8], part), 71), part),
        "beam_newkv": noise(part_splits[7], (BEAMS, 2 * KVH * HD), 1.0, 6.0, ((0, 8), (1, 2))),
    }


def attend(query, own, keys_values, valid):
    beams = query.shape[0]
    query_heads = query.astype(jnp.float32).reshape(beams, KVH, QPK, HD)
    cache = keys_values.astype(jnp.float32).reshape(beams, keys_values.shape[1], KVH, 2, HD)
    own_heads = own.astype(jnp.float32).reshape(beams, KVH, 2, HD)
    scale = HD ** (-0.5)
    scores = jnp.einsum('bgqd,btgd->bgqt', query_heads, cache[:, :, :, 0]) * scale
    scores = jnp.where(valid[:, None, None, :], scores, -jnp.inf)
    own_score = jnp.einsum('bgqd,bgd->bgq', query_heads, own_heads[:, :, 0]) * scale
    top = jnp.maximum(lax.optimization_barrier(jnp.max(scores, axis=-1)), own_score)
    expo = jnp.exp(scores - top[..., None])
    own_expo = jnp.exp(own_score - top)
    total = lax.optimization_barrier(jnp.sum(expo, axis=-1)) + own_expo
    weights = (expo / total[..., None]).astype(jnp.bfloat16)
    own_weight = (own_expo / total).astype(jnp.bfloat16)
    mixed = jnp.einsum('bgqt,btgd->bgqd', weights.astype(jnp.float32), cache[:, :, :, 1])
    mixed = mixed + own_weight.astype(jnp.float32)[..., None] * own_heads[:, :, 1][:, :, None, :]
    return mixed.reshape(beams, KVH * QPK * HD).astype(jnp.bfloat16)

def reference(tokens, norm_gain, kv_weight, lengths, decode_host, beam_counts, beam_query, beam_newkv):
    tok32 = tokens.astype(jnp.float32)
    inverse = lax.rsqrt(lax.optimization_barrier(jnp.mean(tok32 * tok32, axis=1)) + 1e-05)
    scaled = (tok32 * norm_gain.astype(jnp.float32)).astype(jnp.bfloat16)
    projected = jnp.dot(scaled, kv_weight, preferred_element_type=jnp.float32)
    prompt_kv = (projected * inverse[:, None]).astype(jnp.bfloat16)
    lengths = lengths.astype(jnp.int32)
    starts = (jnp.cumsum(lengths, axis=1) - lengths).astype(jnp.int32)
    offsets = jnp.arange(MAXLEN, dtype=jnp.int32)
    local_rows = jnp.clip(starts[:, :, None] + offsets[None, None, :], 0, TOK_DEV - 1)
    devices = jnp.arange(N_SECTION, dtype=jnp.int32)
    rows = (devices[:, None, None] * TOK_DEV + local_rows).astype(jnp.int32)
    valid = offsets[None, None, :] < lengths[:, :, None]
    cache = prompt_kv[rows]
    match = decode_host[:, None, :] == devices[None, :, None]
    source = lax.optimization_barrier(jnp.sum(jnp.where(match, devices[:, None, None], 0), axis=0)).astype(jnp.int32)

    def one_device(pieces):
        counts, sources, query, own = pieces
        ends = jnp.cumsum(counts).astype(jnp.int32)
        beam_index = jnp.arange(BEAM_DEV, dtype=jnp.int32)
        slot = lax.optimization_barrier(jnp.sum((beam_index[:, None] >= ends[None, :]).astype(jnp.int32), axis=1)).astype(jnp.int32)
        prompt_source = sources[slot].astype(jnp.int32)
        return attend(query, own, cache[prompt_source, slot], valid[prompt_source, slot])
    context = lax.map(one_device, (beam_counts.astype(jnp.int32), source, beam_query.reshape(N_SECTION, BEAM_DEV, KVH * QPK * HD), beam_newkv.reshape(N_SECTION, BEAM_DEV, 2 * KVH * HD)))
    return context.reshape(N_SECTION * BEAM_DEV, KVH * QPK * HD)
```

```python
import functools

import jax
import jax.numpy as jnp
from jax import lax
from jax.experimental import pallas as pl
from jax.experimental.pallas import tpu as pltpu
from jax.sharding import PartitionSpec as P

D = 8192
QPK = 8
HD = 128
BMAX = 16
MAXLEN = 96
META = 16
PACK = 8
STEP = 512
VMEM_LIMIT = 48 * 1024 * 1024


def project_kernel(half, tok_ref, gain_ref, w_ref, out_ref, *, with_squares):
    first = pl.program_id(0) == 0
    width = w_ref.shape[1]
    tok = tok_ref[...].astype(jnp.float32)
    scaled = (tok * gain_ref[...].astype(jnp.float32)).astype(jnp.bfloat16)
    part = jnp.dot(scaled, w_ref[...], preferred_element_type=jnp.float32)
    if with_squares:
        sq = tok * tok
        lanes = sq[:, :HD]
        for c in range(HD, sq.shape[1], HD):
            lanes = lanes + sq[:, c : c + HD]

    @pl.when(first)
    def _():
        out_ref[:, :width] = part
        if with_squares:
            out_ref[:, width:] = lanes

    @pl.when(jnp.logical_not(first))
    def _():
        out_ref[:, :width] += part
        if with_squares:
            out_ref[:, width:] += lanes


def project(half, tokens, gain, weight, with_squares):
    rows, depth = tokens.shape
    width = weight.shape[1] // 2
    out_width = width + (HD if with_squares else 0)
    return pl.pallas_call(
        functools.partial(project_kernel, with_squares=with_squares),
        out_shape=jax.ShapeDtypeStruct((rows, out_width), jnp.float32),
        grid_spec=pltpu.PrefetchScalarGridSpec(
            num_scalar_prefetch=1,
            grid=(depth // STEP,),
            in_specs=[
                pl.BlockSpec((rows, STEP), lambda k, half: (0, k)),
                pl.BlockSpec((1, STEP), lambda k, half: (0, k)),
                pl.BlockSpec((STEP, width), lambda k, half: (k, half[0])),
            ],
            out_specs=pl.BlockSpec((rows, out_width), lambda k, half: (0, 0)),
        ),
        compiler_params=pltpu.CompilerParams(vmem_limit_bytes=VMEM_LIMIT),
        cost_estimate=pl.CostEstimate(
            flops=2 * rows * depth * width,
            bytes_accessed=2 * depth * (rows + width) + 4 * rows * out_width,
            transcendentals=0,
        ),
        name="project",
    )(half, tokens, gain, weight)


def pack_kernel(keep_ref, recv_ref, sq_ref, len_ref, host_ref, out_ref):
    rows, width = keep_ref.shape
    prompts = len_ref.shape[1]
    squares = jnp.sum(recv_ref[:, width:] + sq_ref[...], axis=1, keepdims=True)
    inverse = lax.rsqrt(squares / D + 1e-05)
    kv = ((keep_ref[...] + recv_ref[:, :width]) * inverse).astype(jnp.bfloat16)
    lane = lax.broadcasted_iota(jnp.int32, (META, HD), 1)
    row_at = lax.broadcasted_iota(jnp.int32, (MAXLEN, rows), 1)
    row_at = row_at - lax.broadcasted_iota(jnp.int32, (MAXLEN, rows), 0)

    def place(chunk, start):
        picks = []
        for i in range(PACK):
            picks.append((row_at == start).astype(jnp.float32).astype(jnp.bfloat16))
            start = start + len_ref[0, chunk * PACK + i]
        blocks = jnp.dot(
            jnp.concatenate(picks, axis=0), kv, preferred_element_type=jnp.float32
        ).astype(jnp.bfloat16)
        for i in range(PACK):
            slot = chunk * PACK + i
            dest = host_ref[0, slot]
            for g in range(width // HD):
                out_ref[dest, g * MAXLEN : (g + 1) * MAXLEN, :] = blocks[
                    i * MAXLEN : (i + 1) * MAXLEN, g * HD : (g + 1) * HD
                ]
            meta = jnp.where(lane == 0, slot, jnp.where(lane == 1, len_ref[0, slot], 0))
            out_ref[dest, width // HD * MAXLEN :, :] = meta.astype(jnp.float32).astype(jnp.bfloat16)
        return start

    if prompts == PACK:
        place(0, 0)
    else:
        lax.fori_loop(0, prompts // PACK, place, jnp.int32(0))


def pack(keep, recv, send, lengths, decode_host, sections):
    rows, width = keep.shape
    height = width // HD * MAXLEN + META
    smem = pl.BlockSpec(memory_space=pltpu.SMEM)
    return pl.pallas_call(
        pack_kernel,
        out_shape=jax.ShapeDtypeStruct((sections, height, HD), jnp.bfloat16),
        grid=(1,),
        in_specs=[
            pl.BlockSpec((rows, width), lambda i: (0, 0)),
            pl.BlockSpec((rows, width + HD), lambda i: (0, 0)),
            pl.BlockSpec((rows, HD), lambda i: (0, width // HD)),
            smem,
            smem,
        ],
        out_specs=pl.BlockSpec((sections, height, HD), lambda i: (0, 0, 0)),
        compiler_params=pltpu.CompilerParams(vmem_limit_bytes=VMEM_LIMIT),
        name="pack",
    )(keep, recv, send, lengths, decode_host)


def attend_kernel(got_ref, query_ref, own_ref, count_ref, out_ref, q_ref, own32_ref, o_ref, src_ref, len_ref):
    sections = got_ref.shape[0]
    beams = query_ref.shape[0]
    heads = query_ref.shape[1] // HD
    groups = heads // QPK
    base = 2 * groups * MAXLEN
    scale = HD ** (-0.5)
    tail = jnp.zeros((BMAX, HD), jnp.float32)
    for h in range(heads):
        q_ref[h, :beams, :] = query_ref[:, h * HD : (h + 1) * HD].astype(jnp.float32)
        q_ref[h, beams:, :] = tail
    for g in range(2 * groups):
        own32_ref[g, :beams, :] = own_ref[:, g * HD : (g + 1) * HD].astype(jnp.float32)
        own32_ref[g, beams:, :] = tail
    for s in range(sections):
        meta = got_ref[s, base : base + META, :].astype(jnp.float32)
        slot = meta[0, 0].astype(jnp.int32)
        src_ref[slot] = s
        len_ref[slot] = meta[0, 1].astype(jnp.int32)
    lane = lax.broadcasted_iota(jnp.int32, (QPK * BMAX, MAXLEN), 1)

    def prompt(j, start):
        source = src_ref[j]
        live = lane < len_ref[j]
        at = pl.ds(start, BMAX)
        for g in range(groups):
            keys = got_ref[source, 2 * g * MAXLEN : (2 * g + 1) * MAXLEN, :]
            values = got_ref[source, (2 * g + 1) * MAXLEN : (2 * g + 2) * MAXLEN, :]
            q3 = q_ref[g * QPK : (g + 1) * QPK, at, :]
            own_key = own32_ref[2 * g, at, :]
            own_value = own32_ref[2 * g + 1, at, :]
            own_score = jnp.sum(q3 * own_key[None], axis=2, keepdims=True) * scale
            own_score = own_score.reshape(QPK * BMAX, 1)
            q2 = q3.reshape(QPK * BMAX, HD).astype(jnp.bfloat16)
            scores = lax.dot_general(
                q2, keys, (((1,), (1,)), ((), ())), preferred_element_type=jnp.float32
            )
            scores = jnp.where(live, scores * scale, -jnp.inf)
            top = jnp.maximum(jnp.max(scores, axis=1, keepdims=True), own_score)
            expo = jnp.exp(scores - top)
            own_expo = jnp.exp(own_score - top)
            total = jnp.sum(expo, axis=1, keepdims=True) + own_expo
            weights = (expo / total).astype(jnp.bfloat16)
            own_weight = (own_expo / total).astype(jnp.bfloat16).astype(jnp.float32)
            mixed = jnp.dot(weights, values, preferred_element_type=jnp.float32)
            mixed = mixed.reshape(QPK, BMAX, HD)
            mixed = mixed + own_weight.reshape(QPK, BMAX, 1) * own_value[None]
            o_ref[g * QPK : (g + 1) * QPK, at, :] = mixed
        return start + count_ref[0, j]

    if sections <= 8:
        start = 0
        for j in range(sections):
            start = prompt(j, start)
    else:
        lax.fori_loop(0, sections, prompt, jnp.int32(0))
    for h in range(heads):
        out_ref[:, h * HD : (h + 1) * HD] = o_ref[h, :beams, :].astype(jnp.bfloat16)


def attend(got, query, own, counts):
    sections, height, _ = got.shape
    beams, width = query.shape
    heads = width // HD
    return pl.pallas_call(
        attend_kernel,
        out_shape=jax.ShapeDtypeStruct((beams, width), jnp.bfloat16),
        in_specs=[
            pl.BlockSpec(memory_space=pltpu.VMEM),
            pl.BlockSpec(memory_space=pltpu.VMEM),
            pl.BlockSpec(memory_space=pltpu.VMEM),
            pl.BlockSpec(memory_space=pltpu.SMEM),
        ],
        out_specs=pl.BlockSpec(memory_space=pltpu.VMEM),
        scratch_shapes=[
            pltpu.VMEM((heads, beams + BMAX, HD), jnp.float32),
            pltpu.VMEM((own.shape[1] // HD, beams + BMAX, HD), jnp.float32),
            pltpu.VMEM((heads, beams + BMAX, HD), jnp.float32),
            pltpu.SMEM((sections,), jnp.int32),
            pltpu.SMEM((sections,), jnp.int32),
        ],
        compiler_params=pltpu.CompilerParams(vmem_limit_bytes=VMEM_LIMIT),
        name="attend",
    )(got, query, own, counts)


def per_device(tokens, norm_gain, kv_weight, lengths, decode_host, beam_counts, beam_query, beam_newkv):
    sections = lax.axis_size("section")
    mine = lax.axis_index("tensor").astype(jnp.int32).reshape(1)
    gain = norm_gain.reshape(1, -1)
    send = project(1 - mine, tokens, gain, kv_weight, True)
    recv = lax.ppermute(send, "tensor", [(0, 1), (1, 0)])
    keep = project(mine, tokens, gain, kv_weight, False)
    outgoing = pack(keep, recv, send, lengths, decode_host, sections)
    got = lax.all_to_all(outgoing, "section", split_axis=0, concat_axis=0, tiled=True)
    return attend(got, beam_query, beam_newkv, beam_counts)


def solution(mesh):
    rows = ("groups", "section")
    placed = (
        P(rows, "tensor"),
        P("tensor"),
        P("tensor", None),
        P(rows, None),
        P(rows, None),
        P(rows, None),
        P(rows, "tensor"),
        P(rows, "tensor"),
    )
    return jax.shard_map(
        per_device,
        mesh=mesh,
        in_specs=placed,
        out_specs=P(rows, "tensor"),
        check_vma=False,
    )
```

```python
import functools

import jax
import jax.numpy as jnp
from jax import lax
from jax.experimental import pallas as pl
from jax.experimental.pallas import tpu as pltpu
from jax.sharding import PartitionSpec as P

D = 8192
QPK = 8
HD = 128
BMAX = 16
MAXLEN = 96
META = 16
STEP = 512
GROUP = 8
VMEM_LIMIT = 44 * 1024 * 1024

VMEM = pl.BlockSpec(memory_space=pltpu.VMEM)
SMEM = pl.BlockSpec(memory_space=pltpu.SMEM)
HBM = pl.BlockSpec(memory_space=pltpu.HBM)


def weight_copy(w_ref, w_buf, sem, half, c):
    width = w_buf.shape[2]
    columns = pl.ds(pl.multiple_of(half * width, width), width)
    return pltpu.make_async_copy(w_ref.at[pl.ds(c * STEP, STEP), columns], w_buf.at[c], sem.at[c])


def project_send_kernel(half_ref, tok_ref, gain_ref, w_ref, out_ref, scaled_ref, tok_buf, w_buf, tok_sem, w_sem):
    half = half_ref[0]
    steps = w_buf.shape[0]
    width = w_buf.shape[2]

    def token_copy(c):
        return pltpu.make_async_copy(tok_ref.at[:, pl.ds(c * STEP, STEP)], tok_buf.at[c], tok_sem.at[c])

    for c in range(steps):
        token_copy(c).start()
        weight_copy(w_ref, w_buf, w_sem, half, c).start()
    gain = gain_ref[...].astype(jnp.float32)
    for c in range(steps):
        token_copy(c).wait()
        for b in range(STEP // HD):
            at = c * (STEP // HD) + b
            tok = tok_buf[c, :, b * HD : (b + 1) * HD].astype(jnp.float32)
            scaled_ref[:, at * HD : (at + 1) * HD] = (tok * gain[at : at + 1, :]).astype(jnp.bfloat16)
            if at == 0:
                out_ref[:, width:] = tok * tok
            else:
                out_ref[:, width:] += tok * tok
        weight_copy(w_ref, w_buf, w_sem, half, c).wait()
        part = jnp.dot(
            scaled_ref[:, c * STEP : (c + 1) * STEP], w_buf[c], preferred_element_type=jnp.float32
        )
        if c == 0:
            out_ref[:, :width] = part
        else:
            out_ref[:, :width] += part


def project_keep_kernel(half_ref, scaled_ref, w_ref, out_ref, w_buf, w_sem):
    half = half_ref[0]
    steps = w_buf.shape[0]
    for c in range(steps):
        weight_copy(w_ref, w_buf, w_sem, half, c).start()
    for c in range(steps):
        weight_copy(w_ref, w_buf, w_sem, half, c).wait()
        part = jnp.dot(
            scaled_ref[:, c * STEP : (c + 1) * STEP], w_buf[c], preferred_element_type=jnp.float32
        )
        if c == 0:
            out_ref[...] = part
        else:
            out_ref[...] += part


def project_cost(rows, depth, width):
    return pl.CostEstimate(
        flops=2 * rows * depth * width,
        bytes_accessed=2 * depth * (rows + width) + 4 * rows * width,
        transcendentals=0,
    )


def project_send(half, tokens, gain, weight):
    rows, depth = tokens.shape
    width = weight.shape[1] // 2
    steps = depth // STEP
    return pl.pallas_call(
        project_send_kernel,
        out_shape=(
            jax.ShapeDtypeStruct((rows, width + HD), jnp.float32),
            jax.ShapeDtypeStruct((rows, depth), jnp.bfloat16),
        ),
        in_specs=[SMEM, HBM, VMEM, HBM],
        out_specs=(VMEM, VMEM),
        scratch_shapes=[
            pltpu.VMEM((steps, rows, STEP), jnp.bfloat16),
            pltpu.VMEM((steps, STEP, width), jnp.bfloat16),
            pltpu.SemaphoreType.DMA((steps,)),
            pltpu.SemaphoreType.DMA((steps,)),
        ],
        compiler_params=pltpu.CompilerParams(vmem_limit_bytes=VMEM_LIMIT),
        cost_estimate=project_cost(rows, depth, width),
        name="project_send",
    )(half, tokens, gain, weight)


def project_keep(half, scaled, weight):
    rows, depth = scaled.shape
    width = weight.shape[1] // 2
    steps = depth // STEP
    return pl.pallas_call(
        project_keep_kernel,
        out_shape=jax.ShapeDtypeStruct((rows, width), jnp.float32),
        in_specs=[SMEM, VMEM, HBM],
        out_specs=VMEM,
        scratch_shapes=[
            pltpu.VMEM((steps, STEP, width), jnp.bfloat16),
            pltpu.SemaphoreType.DMA((steps,)),
        ],
        compiler_params=pltpu.CompilerParams(vmem_limit_bytes=VMEM_LIMIT),
        cost_estimate=project_cost(rows, depth, width),
        name="project_keep",
    )(half, scaled, weight)


def pack_kernel(me_ref, keep_ref, recv_ref, send_ref, len_ref, host_ref, *refs):
    outs, slot_ref, start_ref = refs[:-2], refs[-2], refs[-1]
    rows, width = keep_ref.shape
    prompts = len_ref.shape[1]
    me = me_ref[0]
    start = 0
    for i in range(prompts):
        turn = host_ref[0, i] ^ me
        slot_ref[turn] = i
        start_ref[turn] = start
        start = start + len_ref[0, i]
    squares = jnp.sum(recv_ref[:, width:] + send_ref[:, width:], axis=1, keepdims=True)
    inverse = lax.rsqrt(squares / D + 1e-05)
    kv = ((keep_ref[...] + recv_ref[:, :width]) * inverse).astype(jnp.bfloat16)
    lane = lax.broadcasted_iota(jnp.int32, (META, HD), 1)
    row_at = lax.broadcasted_iota(jnp.int32, (MAXLEN, rows), 1)
    row_at = row_at - lax.broadcasted_iota(jnp.int32, (MAXLEN, rows), 0)
    for base in range(0, prompts, GROUP):
        turns = range(base, min(base + GROUP, prompts))
        picks = [(row_at == start_ref[k]).astype(jnp.float32).astype(jnp.bfloat16) for k in turns]
        blocks = jnp.dot(
            jnp.concatenate(picks, axis=0), kv, preferred_element_type=jnp.float32
        ).astype(jnp.bfloat16)
        for k in turns:
            at = (k - base) * MAXLEN
            for g in range(width // HD):
                outs[k][g * MAXLEN : (g + 1) * MAXLEN, :] = blocks[
                    at : at + MAXLEN, g * HD : (g + 1) * HD
                ]
            slot = slot_ref[k]
            meta = jnp.where(lane == 0, slot, jnp.where(lane == 1, len_ref[0, slot], 0))
            outs[k][width // HD * MAXLEN :, :] = meta.astype(jnp.float32).astype(jnp.bfloat16)


def pack(me, keep, recv, send, lengths, decode_host, sections):
    width = keep.shape[1]
    height = width // HD * MAXLEN + META
    return pl.pallas_call(
        pack_kernel,
        out_shape=[jax.ShapeDtypeStruct((height, HD), jnp.bfloat16)] * sections,
        in_specs=[SMEM, VMEM, VMEM, VMEM, SMEM, SMEM],
        out_specs=[VMEM] * sections,
        scratch_shapes=[pltpu.SMEM((sections,), jnp.int32), pltpu.SMEM((sections,), jnp.int32)],
        compiler_params=pltpu.CompilerParams(vmem_limit_bytes=VMEM_LIMIT),
        name="pack",
    )(me, keep, recv, send, lengths, decode_host)


def attend_blocks(blocks, count_ref, q_ref, score_ref, value_ref, acc_ref):
    groups = q_ref.shape[0] // QPK
    scale = HD ** (-0.5)
    flat = QPK * BMAX
    lane = lax.broadcasted_iota(jnp.int32, (flat, MAXLEN), 1)
    beam = lax.broadcasted_iota(jnp.int32, (QPK, BMAX, HD), 1)
    work = []
    for block in blocks:
        meta = block[2 * groups * MAXLEN :, :].astype(jnp.float32)
        slot = meta[0, 0].astype(jnp.int32)
        length = meta[0, 1].astype(jnp.int32)
        start = 0
        for i in range(count_ref.shape[1]):
            start = start + jnp.where(i < slot, count_ref[0, i], 0)
        for g in range(groups):
            work.append((block, g, length, pl.ds(start, BMAX), count_ref[0, slot]))
    scores = []
    for block, g, length, at, count in work:
        q = q_ref[g * QPK : (g + 1) * QPK, at, :].reshape(flat, HD).astype(jnp.bfloat16)
        keys = block[2 * g * MAXLEN : (2 * g + 1) * MAXLEN, :]
        raw = lax.dot_general(q, keys, (((1,), (1,)), ((), ())), preferred_element_type=jnp.float32)
        scores.append(jnp.where(lane < length, raw * scale, -jnp.inf))
    tops, owns = [], []
    for (block, g, length, at, count), score in zip(work, scores):
        own = score_ref[g * QPK : (g + 1) * QPK, at, :].reshape(flat, HD)[:, :1]
        owns.append(own)
        tops.append(jnp.maximum(jnp.max(score, axis=1, keepdims=True), own))
    expos = [jnp.exp(score - top) for score, top in zip(scores, tops)]
    own_expos = [jnp.exp(own - top) for own, top in zip(owns, tops)]
    totals = [jnp.sum(e, axis=1, keepdims=True) + o for e, o in zip(expos, own_expos)]
    weights = [(e / t).astype(jnp.bfloat16) for e, t in zip(expos, totals)]
    own_weights = [(o / t).astype(jnp.bfloat16).astype(jnp.float32) for o, t in zip(own_expos, totals)]
    mixes = []
    for (block, g, length, at, count), weight in zip(work, weights):
        values = block[(2 * g + 1) * MAXLEN : (2 * g + 2) * MAXLEN, :]
        mixes.append(jnp.dot(weight, values, preferred_element_type=jnp.float32))
    for (block, g, length, at, count), mix, own in zip(work, mixes, own_weights):
        own = own.reshape(QPK, BMAX, 1) * value_ref[g, at, :][None]
        heads = slice(g * QPK, (g + 1) * QPK)
        acc_ref[heads, at, :] = jnp.where(
            beam < count, mix.reshape(QPK, BMAX, HD) + own, acc_ref[heads, at, :]
        )


def first_kernel(query_ref, own_ref, count_ref, block_ref, q_ref, score_ref, value_ref, acc_ref):
    beams = query_ref.shape[0]
    heads = query_ref.shape[1] // HD
    scale = HD ** (-0.5)
    tail = jnp.zeros((BMAX, HD), jnp.float32)
    for g in range(heads // QPK):
        key = own_ref[:, 2 * g * HD : (2 * g + 1) * HD].astype(jnp.float32)
        value_ref[g, :beams, :] = own_ref[:, (2 * g + 1) * HD : (2 * g + 2) * HD].astype(jnp.float32)
        value_ref[g, beams:, :] = tail
        for h in range(g * QPK, (g + 1) * QPK):
            q = query_ref[:, h * HD : (h + 1) * HD].astype(jnp.float32)
            q_ref[h, :beams, :] = q
            q_ref[h, beams:, :] = tail
            score = jnp.sum(q * key, axis=1, keepdims=True) * scale
            score_ref[h, :beams, :] = jnp.broadcast_to(score, (beams, HD))
            score_ref[h, beams:, :] = tail
    acc_ref[...] = jnp.zeros_like(acc_ref)
    attend_blocks([block_ref], count_ref, q_ref, score_ref, value_ref, acc_ref)


def attend_first(query, own, counts, block):
    beams, width = query.shape
    heads = width // HD
    tall = jax.ShapeDtypeStruct((heads, beams + BMAX, HD), jnp.float32)
    return pl.pallas_call(
        first_kernel,
        out_shape=(tall, tall, jax.ShapeDtypeStruct((heads // QPK, beams + BMAX, HD), jnp.float32), tall),
        in_specs=[VMEM, VMEM, SMEM, VMEM],
        out_specs=(VMEM,) * 4,
        compiler_params=pltpu.CompilerParams(vmem_limit_bytes=VMEM_LIMIT),
        cost_estimate=pl.CostEstimate(flops=1 << 24, bytes_accessed=4 << 20, transcendentals=0),
        name="attend_first",
    )(query, own, counts, block)


def later_kernel(count_ref, q_ref, score_ref, value_ref, acc_in, *refs, n_blocks, last):
    blocks, rest = refs[:n_blocks], refs[n_blocks:]
    acc_ref = rest[0]
    for base in range(0, n_blocks, GROUP // 2):
        attend_blocks(blocks[base : base + GROUP // 2], count_ref, q_ref, score_ref, value_ref, acc_ref)
    if last:
        out_ref = rest[1]
        beams = out_ref.shape[0]
        for h in range(acc_ref.shape[0]):
            out_ref[:, h * HD : (h + 1) * HD] = acc_ref[h, :beams, :].astype(jnp.bfloat16)


def attend_later(counts, q, score, value, acc, blocks, out_shape):
    last = out_shape is not None
    shapes = [jax.ShapeDtypeStruct(acc.shape, acc.dtype)]
    if last:
        shapes.append(out_shape)
    return pl.pallas_call(
        functools.partial(later_kernel, n_blocks=len(blocks), last=last),
        out_shape=shapes,
        in_specs=[SMEM] + [VMEM] * (4 + len(blocks)),
        out_specs=[VMEM] * len(shapes),
        input_output_aliases={4: 0},
        compiler_params=pltpu.CompilerParams(vmem_limit_bytes=VMEM_LIMIT),
        cost_estimate=pl.CostEstimate(flops=1 << 24, bytes_accessed=4 << 20, transcendentals=0),
        name="attend_last" if last else "attend_more",
    )(counts, q, score, value, acc, *blocks)


def per_device(tokens, norm_gain, kv_weight, lengths, decode_host, beam_counts, beam_query, beam_newkv):
    sections = lax.axis_size("section")
    mine = lax.axis_index("tensor").astype(jnp.int32).reshape(1)
    me = lax.axis_index("section").astype(jnp.int32).reshape(1)
    gain = norm_gain.reshape(-1, HD)
    send, scaled = project_send(1 - mine, tokens, gain, kv_weight)
    recv = lax.ppermute(send, "tensor", [(0, 1), (1, 0)])
    keep = project_keep(mine, scaled, kv_weight)
    blocks = pack(me, keep, recv, send, lengths, decode_host, sections)
    got = {}
    for k in range(1, sections):
        got[k] = lax.ppermute(blocks[k], "section", [(s, s ^ k) for s in range(sections)])
    q, score, value, acc = attend_first(beam_query, beam_newkv, beam_counts, blocks[0])
    cut = sections // 2
    early = [got[k] for k in range(sections - 1, cut, -1)]
    late = [got[k] for k in range(cut, 0, -1)]
    (acc,) = attend_later(beam_counts, q, score, value, acc, early, None)
    out_shape = jax.ShapeDtypeStruct(beam_query.shape, jnp.bfloat16)
    return attend_later(beam_counts, q, score, value, acc, late, out_shape)[1]


def solution(mesh):
    rows = ("groups", "section")
    placed = (
        P(rows, "tensor"),
        P("tensor"),
        P("tensor", None),
        P(rows, None),
        P(rows, None),
        P(rows, None),
        P(rows, "tensor"),
        P(rows, "tensor"),
    )
    return jax.shard_map(
        per_device,
        mesh=mesh,
        in_specs=placed,
        out_specs=P(rows, "tensor"),
        check_vma=False,
    )
```

```python
import functools

import jax
import jax.numpy as jnp
from jax import lax
from jax.experimental import pallas as pl
from jax.experimental.pallas import tpu as pltpu
from jax.sharding import PartitionSpec as P

D = 8192
QPK = 8
HD = 128
BMAX = 16
MAXLEN = 96
META = 16
STEP = 512
GROUP = 8
VMEM_LIMIT = 44 * 1024 * 1024
PROJECT_LIMIT = 52800000

VMEM = pl.BlockSpec(memory_space=pltpu.VMEM)
SMEM = pl.BlockSpec(memory_space=pltpu.SMEM)
HBM = pl.BlockSpec(memory_space=pltpu.HBM)


def weight_copy(w_ref, w_buf, sem, half, c):
    width = w_buf.shape[2]
    columns = pl.ds(pl.multiple_of(half * width, width), width)
    return pltpu.make_async_copy(w_ref.at[pl.ds(c * STEP, STEP), columns], w_buf.at[c], sem.at[c])


def project_send_kernel(half_ref, tok_ref, gain_ref, w_ref, out_ref, scaled_ref, tok_buf, w_buf, tok_sem, w_sem):
    half = half_ref[0]
    steps = w_buf.shape[0]
    width = w_buf.shape[2]
    blocks = STEP // HD

    def token_copy(c):
        return pltpu.make_async_copy(tok_ref.at[:, pl.ds(c * STEP, STEP)], tok_buf.at[c], tok_sem.at[c])

    def scale(c):
        token_copy(c).wait()
        squares = None
        for b in range(blocks):
            at = c * blocks + b
            tok = tok_buf[c, :, b * HD : (b + 1) * HD].astype(jnp.float32)
            scaled_ref[:, at * HD : (at + 1) * HD] = (tok * gain[at : at + 1, :]).astype(jnp.bfloat16)
            squares = tok * tok if squares is None else squares + tok * tok
        if c == 0:
            out_ref[:, width:] = squares
        else:
            out_ref[:, width:] += squares

    for c in range(steps):
        token_copy(c).start()
        weight_copy(w_ref, w_buf, w_sem, half, c).start()
    gain = gain_ref[...].astype(jnp.float32)
    scale(0)
    for c in range(steps):
        weight_copy(w_ref, w_buf, w_sem, half, c).wait()
        if c + 1 < steps:
            scale(c + 1)
        part = jnp.dot(
            scaled_ref[:, c * STEP : (c + 1) * STEP], w_buf[c], preferred_element_type=jnp.float32
        )
        if c == 0:
            out_ref[:, :width] = part
        else:
            out_ref[:, :width] += part


def project_keep_kernel(half_ref, scaled_ref, w_ref, out_ref, w_buf, w_sem):
    half = half_ref[0]
    steps = w_buf.shape[0]
    for c in range(steps):
        weight_copy(w_ref, w_buf, w_sem, half, c).start()
    for c in range(steps):
        weight_copy(w_ref, w_buf, w_sem, half, c).wait()
        part = jnp.dot(
            scaled_ref[:, c * STEP : (c + 1) * STEP], w_buf[c], preferred_element_type=jnp.float32
        )
        if c == 0:
            out_ref[...] = part
        else:
            out_ref[...] += part


def project_cost(rows, depth, width):
    return pl.CostEstimate(
        flops=2 * rows * depth * width,
        bytes_accessed=2 * depth * (rows + width) + 4 * rows * width,
        transcendentals=0,
    )


def project_send(half, tokens, gain, weight):
    rows, depth = tokens.shape
    width = weight.shape[1] // 2
    steps = depth // STEP
    return pl.pallas_call(
        project_send_kernel,
        out_shape=(
            jax.ShapeDtypeStruct((rows, width + HD), jnp.float32),
            jax.ShapeDtypeStruct((rows, depth), jnp.bfloat16),
        ),
        in_specs=[SMEM, HBM, VMEM, HBM],
        out_specs=(VMEM, VMEM),
        scratch_shapes=[
            pltpu.VMEM((steps, rows, STEP), jnp.bfloat16),
            pltpu.VMEM((steps, STEP, width), jnp.bfloat16),
            pltpu.SemaphoreType.DMA((steps,)),
            pltpu.SemaphoreType.DMA((steps,)),
        ],
        compiler_params=pltpu.CompilerParams(vmem_limit_bytes=PROJECT_LIMIT),
        cost_estimate=project_cost(rows, depth, width),
        name="project_send",
    )(half, tokens, gain, weight)


def project_keep(half, scaled, weight):
    rows, depth = scaled.shape
    width = weight.shape[1] // 2
    steps = depth // STEP
    return pl.pallas_call(
        project_keep_kernel,
        out_shape=jax.ShapeDtypeStruct((rows, width), jnp.float32),
        in_specs=[SMEM, VMEM, HBM],
        out_specs=VMEM,
        scratch_shapes=[
            pltpu.VMEM((steps, STEP, width), jnp.bfloat16),
            pltpu.SemaphoreType.DMA((steps,)),
        ],
        compiler_params=pltpu.CompilerParams(vmem_limit_bytes=VMEM_LIMIT),
        cost_estimate=project_cost(rows, depth, width),
        name="project_keep",
    )(half, scaled, weight)


def pack_kernel(me_ref, keep_ref, recv_ref, send_ref, len_ref, host_ref, *refs):
    outs, slot_ref, start_ref = refs[:-2], refs[-2], refs[-1]
    rows, width = keep_ref.shape
    prompts = len_ref.shape[1]
    me = me_ref[0]
    start = 0
    for i in range(prompts):
        turn = host_ref[0, i] ^ me
        slot_ref[turn] = i
        start_ref[turn] = start
        start = start + len_ref[0, i]
    squares = jnp.sum(recv_ref[:, width:] + send_ref[:, width:], axis=1, keepdims=True)
    inverse = lax.rsqrt(squares / D + 1e-05)
    kv = ((keep_ref[...] + recv_ref[:, :width]) * inverse).astype(jnp.bfloat16)
    lane = lax.broadcasted_iota(jnp.int32, (META, HD), 1)
    row_at = lax.broadcasted_iota(jnp.int32, (MAXLEN, rows), 1)
    row_at = row_at - lax.broadcasted_iota(jnp.int32, (MAXLEN, rows), 0)
    for base in range(0, prompts, GROUP):
        turns = range(base, min(base + GROUP, prompts))
        picks = [(row_at == start_ref[k]).astype(jnp.float32).astype(jnp.bfloat16) for k in turns]
        blocks = jnp.dot(
            jnp.concatenate(picks, axis=0), kv, preferred_element_type=jnp.float32
        ).astype(jnp.bfloat16)
        for k in turns:
            at = (k - base) * MAXLEN
            for g in range(width // HD):
                outs[k][g * MAXLEN : (g + 1) * MAXLEN, :] = blocks[
                    at : at + MAXLEN, g * HD : (g + 1) * HD
                ]
            slot = slot_ref[k]
            meta = jnp.where(lane == 0, slot, jnp.where(lane == 1, len_ref[0, slot], 0))
            outs[k][width // HD * MAXLEN :, :] = meta.astype(jnp.float32).astype(jnp.bfloat16)


def pack(me, keep, recv, send, lengths, decode_host, sections):
    width = keep.shape[1]
    height = width // HD * MAXLEN + META
    return pl.pallas_call(
        pack_kernel,
        out_shape=[jax.ShapeDtypeStruct((height, HD), jnp.bfloat16)] * sections,
        in_specs=[SMEM, VMEM, VMEM, VMEM, SMEM, SMEM],
        out_specs=[VMEM] * sections,
        scratch_shapes=[pltpu.SMEM((sections,), jnp.int32), pltpu.SMEM((sections,), jnp.int32)],
        compiler_params=pltpu.CompilerParams(vmem_limit_bytes=VMEM_LIMIT),
        name="pack",
    )(me, keep, recv, send, lengths, decode_host)


def attend_blocks(blocks, count_ref, q_ref, score_ref, value_ref, acc_ref):
    groups = q_ref.shape[0] // QPK
    scale = HD ** (-0.5)
    flat = QPK * BMAX
    lane = lax.broadcasted_iota(jnp.int32, (flat, MAXLEN), 1)
    beam = lax.broadcasted_iota(jnp.int32, (QPK, BMAX, HD), 1)
    work = []
    for block in blocks:
        meta = block[2 * groups * MAXLEN :, :].astype(jnp.float32)
        slot = meta[0, 0].astype(jnp.int32)
        length = meta[0, 1].astype(jnp.int32)
        start = 0
        for i in range(count_ref.shape[1]):
            start = start + jnp.where(i < slot, count_ref[0, i], 0)
        for g in range(groups):
            work.append((block, g, length, pl.ds(start, BMAX), count_ref[0, slot]))
    scores = []
    for block, g, length, at, count in work:
        q = q_ref[g * QPK : (g + 1) * QPK, at, :].reshape(flat, HD).astype(jnp.bfloat16)
        keys = block[2 * g * MAXLEN : (2 * g + 1) * MAXLEN, :]
        raw = lax.dot_general(q, keys, (((1,), (1,)), ((), ())), preferred_element_type=jnp.float32)
        scores.append(jnp.where(lane < length, raw * scale, -jnp.inf))
    tops, owns = [], []
    for (block, g, length, at, count), score in zip(work, scores):
        own = score_ref[g * QPK : (g + 1) * QPK, at, :].reshape(flat, HD)[:, :1]
        owns.append(own)
        tops.append(jnp.maximum(jnp.max(score, axis=1, keepdims=True), own))
    expos = [jnp.exp(score - top) for score, top in zip(scores, tops)]
    own_expos = [jnp.exp(own - top) for own, top in zip(owns, tops)]
    totals = [jnp.sum(e, axis=1, keepdims=True) + o for e, o in zip(expos, own_expos)]
    weights = [(e / t).astype(jnp.bfloat16) for e, t in zip(expos, totals)]
    own_weights = [(o / t).astype(jnp.bfloat16).astype(jnp.float32) for o, t in zip(own_expos, totals)]
    mixes = []
    for (block, g, length, at, count), weight in zip(work, weights):
        values = block[(2 * g + 1) * MAXLEN : (2 * g + 2) * MAXLEN, :]
        mixes.append(jnp.dot(weight, values, preferred_element_type=jnp.float32))
    for (block, g, length, at, count), mix, own in zip(work, mixes, own_weights):
        own = own.reshape(QPK, BMAX, 1) * value_ref[g, at, :][None]
        heads = slice(g * QPK, (g + 1) * QPK)
        acc_ref[heads, at, :] = jnp.where(
            beam < count, mix.reshape(QPK, BMAX, HD) + own, acc_ref[heads, at, :]
        )


def first_kernel(query_ref, own_ref, count_ref, block_ref, q_ref, score_ref, value_ref, acc_ref):
    beams = query_ref.shape[0]
    heads = query_ref.shape[1] // HD
    scale = HD ** (-0.5)
    tail = jnp.zeros((BMAX, HD), jnp.float32)
    for g in range(heads // QPK):
        key = own_ref[:, 2 * g * HD : (2 * g + 1) * HD].astype(jnp.float32)
        value_ref[g, :beams, :] = own_ref[:, (2 * g + 1) * HD : (2 * g + 2) * HD].astype(jnp.float32)
        value_ref[g, beams:, :] = tail
        for h in range(g * QPK, (g + 1) * QPK):
            q = query_ref[:, h * HD : (h + 1) * HD].astype(jnp.float32)
            q_ref[h, :beams, :] = q
            q_ref[h, beams:, :] = tail
            score = jnp.sum(q * key, axis=1, keepdims=True) * scale
            score_ref[h, :beams, :] = jnp.broadcast_to(score, (beams, HD))
            score_ref[h, beams:, :] = tail
    acc_ref[...] = jnp.zeros_like(acc_ref)
    attend_blocks([block_ref], count_ref, q_ref, score_ref, value_ref, acc_ref)


def attend_first(query, own, counts, block):
    beams, width = query.shape
    heads = width // HD
    tall = jax.ShapeDtypeStruct((heads, beams + BMAX, HD), jnp.float32)
    return pl.pallas_call(
        first_kernel,
        out_shape=(tall, tall, jax.ShapeDtypeStruct((heads // QPK, beams + BMAX, HD), jnp.float32), tall),
        in_specs=[VMEM, VMEM, SMEM, VMEM],
        out_specs=(VMEM,) * 4,
        compiler_params=pltpu.CompilerParams(vmem_limit_bytes=VMEM_LIMIT),
        cost_estimate=pl.CostEstimate(flops=1 << 24, bytes_accessed=4 << 20, transcendentals=0),
        name="attend_first",
    )(query, own, counts, block)


def later_kernel(count_ref, q_ref, score_ref, value_ref, acc_in, *refs, n_blocks, last):
    blocks, rest = refs[:n_blocks], refs[n_blocks:]
    acc_ref = rest[0]
    for base in range(0, n_blocks, GROUP // 2):
        attend_blocks(blocks[base : base + GROUP // 2], count_ref, q_ref, score_ref, value_ref, acc_ref)
    if last:
        out_ref = rest[1]
        beams = out_ref.shape[0]
        for h in range(acc_ref.shape[0]):
            out_ref[:, h * HD : (h + 1) * HD] = acc_ref[h, :beams, :].astype(jnp.bfloat16)


def attend_later(counts, q, score, value, acc, blocks, out_shape):
    last = out_shape is not None
    shapes = [jax.ShapeDtypeStruct(acc.shape, acc.dtype)]
    if last:
        shapes.append(out_shape)
    return pl.pallas_call(
        functools.partial(later_kernel, n_blocks=len(blocks), last=last),
        out_shape=shapes,
        in_specs=[SMEM] + [VMEM] * (4 + len(blocks)),
        out_specs=[VMEM] * len(shapes),
        input_output_aliases={4: 0},
        compiler_params=pltpu.CompilerParams(vmem_limit_bytes=VMEM_LIMIT),
        cost_estimate=pl.CostEstimate(flops=1 << 24, bytes_accessed=4 << 20, transcendentals=0),
        name="attend_last" if last else "attend_more",
    )(counts, q, score, value, acc, *blocks)


def per_device(tokens, norm_gain, kv_weight, lengths, decode_host, beam_counts, beam_query, beam_newkv):
    sections = lax.axis_size("section")
    mine = lax.axis_index("tensor").astype(jnp.int32).reshape(1)
    me = lax.axis_index("section").astype(jnp.int32).reshape(1)
    gain = norm_gain.reshape(-1, HD)
    send, scaled = project_send(1 - mine, tokens, gain, kv_weight)
    recv = lax.ppermute(send, "tensor", [(0, 1), (1, 0)])
    keep = project_keep(mine, scaled, kv_weight)
    blocks = pack(me, keep, recv, send, lengths, decode_host, sections)
    got = {}
    for k in range(1, sections):
        got[k] = lax.ppermute(blocks[k], "section", [(s, s ^ k) for s in range(sections)])
    q, score, value, acc = attend_first(beam_query, beam_newkv, beam_counts, blocks[0])
    cut = sections // 2
    near = [k for k in range(1, cut)]
    order = [sections - 1] + [k for pair in zip(range(sections - 2, cut, -1), near) for k in pair]
    order = order + [near[-1], cut]
    early = [got[k] for k in order[:-2]]
    late = [got[k] for k in order[-2:]]
    (acc,) = attend_later(beam_counts, q, score, value, acc, early, None)
    out_shape = jax.ShapeDtypeStruct(beam_query.shape, jnp.bfloat16)
    return attend_later(beam_counts, q, score, value, acc, late, out_shape)[1]


def solution(mesh):
    rows = ("groups", "section")
    placed = (
        P(rows, "tensor"),
        P("tensor"),
        P("tensor", None),
        P(rows, None),
        P(rows, None),
        P(rows, None),
        P(rows, "tensor"),
        P(rows, "tensor"),
    )
    return jax.shard_map(
        per_device,
        mesh=mesh,
        in_specs=placed,
        out_specs=P(rows, "tensor"),
        check_vma=False,
    )
```

```python
import functools

import jax
import jax.numpy as jnp
from jax import lax
from jax.experimental import pallas as pl
from jax.experimental.pallas import tpu as pltpu
from jax.sharding import PartitionSpec as P

D = 8192
QPK = 8
HD = 128
BMAX = 16
MAXLEN = 96
META = 8
STEP = 512
GROUP = 8
ORDER = (7, 3, 6, 2, 5, 1, 4)
VMEM_LIMIT = 44 * 1024 * 1024
PROJECT_LIMIT = 52800000

VMEM = pl.BlockSpec(memory_space=pltpu.VMEM)
SMEM = pl.BlockSpec(memory_space=pltpu.SMEM)
HBM = pl.BlockSpec(memory_space=pltpu.HBM)


def weight_copy(w_ref, w_buf, sem, half, c):
    width = w_buf.shape[2]
    columns = pl.ds(pl.multiple_of(half * width, width), width)
    return pltpu.make_async_copy(w_ref.at[pl.ds(c * STEP, STEP), columns], w_buf.at[c], sem.at[c])


def project_send_kernel(half_ref, tok_ref, gain_ref, w_ref, out_ref, scaled_ref, tok_buf, w_buf, tok_sem, w_sem):
    half = half_ref[0]
    steps = w_buf.shape[0]
    width = w_buf.shape[2]
    blocks = STEP // HD

    def token_copy(c):
        return pltpu.make_async_copy(tok_ref.at[:, pl.ds(c * STEP, STEP)], tok_buf.at[c], tok_sem.at[c])

    def scale(c):
        token_copy(c).wait()
        squares = None
        for b in range(blocks):
            at = c * blocks + b
            tok = tok_buf[c, :, b * HD : (b + 1) * HD].astype(jnp.float32)
            scaled_ref[:, at * HD : (at + 1) * HD] = (tok * gain[at : at + 1, :]).astype(jnp.bfloat16)
            squares = tok * tok if squares is None else squares + tok * tok
        if c == 0:
            out_ref[:, width:] = squares
        else:
            out_ref[:, width:] += squares

    for c in range(steps):
        token_copy(c).start()
        weight_copy(w_ref, w_buf, w_sem, half, c).start()
    gain = gain_ref[...].astype(jnp.float32)
    scale(0)
    for c in range(steps):
        weight_copy(w_ref, w_buf, w_sem, half, c).wait()
        if c + 1 < steps:
            scale(c + 1)
        part = jnp.dot(
            scaled_ref[:, c * STEP : (c + 1) * STEP], w_buf[c], preferred_element_type=jnp.float32
        )
        if c == 0:
            out_ref[:, :width] = part
        else:
            out_ref[:, :width] += part


def project_keep_kernel(half_ref, scaled_ref, w_ref, out_ref, w_buf, w_sem):
    half = half_ref[0]
    steps = w_buf.shape[0]
    for c in range(steps):
        weight_copy(w_ref, w_buf, w_sem, half, c).start()
    for c in range(steps):
        weight_copy(w_ref, w_buf, w_sem, half, c).wait()
        part = jnp.dot(
            scaled_ref[:, c * STEP : (c + 1) * STEP], w_buf[c], preferred_element_type=jnp.float32
        )
        if c == 0:
            out_ref[...] = part
        else:
            out_ref[...] += part


def project_cost(rows, depth, width):
    return pl.CostEstimate(
        flops=2 * rows * depth * width,
        bytes_accessed=2 * depth * (rows + width) + 4 * rows * width,
        transcendentals=0,
    )


def project_send(half, tokens, gain, weight):
    rows, depth = tokens.shape
    width = weight.shape[1] // 2
    steps = depth // STEP
    return pl.pallas_call(
        project_send_kernel,
        out_shape=(
            jax.ShapeDtypeStruct((rows, width + HD), jnp.float32),
            jax.ShapeDtypeStruct((rows, depth), jnp.bfloat16),
        ),
        in_specs=[SMEM, HBM, VMEM, HBM],
        out_specs=(VMEM, VMEM),
        scratch_shapes=[
            pltpu.VMEM((steps, rows, STEP), jnp.bfloat16),
            pltpu.VMEM((steps, STEP, width), jnp.bfloat16),
            pltpu.SemaphoreType.DMA((steps,)),
            pltpu.SemaphoreType.DMA((steps,)),
        ],
        compiler_params=pltpu.CompilerParams(vmem_limit_bytes=PROJECT_LIMIT),
        cost_estimate=project_cost(rows, depth, width),
        name="project_send",
    )(half, tokens, gain, weight)


def project_keep(half, scaled, weight):
    rows, depth = scaled.shape
    width = weight.shape[1] // 2
    steps = depth // STEP
    return pl.pallas_call(
        project_keep_kernel,
        out_shape=jax.ShapeDtypeStruct((rows, width), jnp.float32),
        in_specs=[SMEM, VMEM, HBM],
        out_specs=VMEM,
        scratch_shapes=[
            pltpu.VMEM((steps, STEP, width), jnp.bfloat16),
            pltpu.SemaphoreType.DMA((steps,)),
        ],
        compiler_params=pltpu.CompilerParams(vmem_limit_bytes=VMEM_LIMIT),
        cost_estimate=project_cost(rows, depth, width),
        name="project_keep",
    )(half, scaled, weight)


def pack_blocks(turns, kv, me, len_ref, host_ref, outs, slot_ref, start_ref):
    rows, width = kv.shape
    start = 0
    for i in range(len_ref.shape[1]):
        turn = host_ref[0, i] ^ me
        slot_ref[turn] = i
        start_ref[turn] = start
        start = start + len_ref[0, i]
    lane = lax.broadcasted_iota(jnp.int32, (META, HD), 1)
    row_at = lax.broadcasted_iota(jnp.int32, (MAXLEN, rows), 1)
    row_at = row_at - lax.broadcasted_iota(jnp.int32, (MAXLEN, rows), 0)
    for base in range(0, len(turns), GROUP):
        part = turns[base : base + GROUP]
        picks = [(row_at == start_ref[k]).astype(jnp.float32).astype(jnp.bfloat16) for k in part]
        blocks = jnp.dot(
            jnp.concatenate(picks, axis=0), kv, preferred_element_type=jnp.float32
        ).astype(jnp.bfloat16)
        for i, k in enumerate(part):
            out = outs[base + i]
            for g in range(width // HD):
                out[g * MAXLEN : (g + 1) * MAXLEN, :] = blocks[
                    i * MAXLEN : (i + 1) * MAXLEN, g * HD : (g + 1) * HD
                ]
            slot = slot_ref[k]
            meta = jnp.where(lane == 0, slot, jnp.where(lane == 1, len_ref[0, slot], 0))
            out[width // HD * MAXLEN :, :] = meta.astype(jnp.float32).astype(jnp.bfloat16)


def pack_first_kernel(me_ref, keep_ref, recv_ref, send_ref, len_ref, host_ref, kv_ref, *refs, turns):
    width = keep_ref.shape[1]
    squares = jnp.sum(recv_ref[:, width:] + send_ref[:, width:], axis=1, keepdims=True)
    inverse = lax.rsqrt(squares / D + 1e-05)
    kv = ((keep_ref[...] + recv_ref[:, :width]) * inverse).astype(jnp.bfloat16)
    kv_ref[...] = kv
    pack_blocks(turns, kv, me_ref[0], len_ref, host_ref, refs[:-2], refs[-2], refs[-1])


def pack_rest_kernel(me_ref, kv_ref, len_ref, host_ref, *refs, turns):
    pack_blocks(turns, kv_ref[...], me_ref[0], len_ref, host_ref, refs[:-2], refs[-2], refs[-1])


def pack(me, keep, recv, send, lengths, decode_host, sections, turns):
    rows, width = keep.shape
    block = jax.ShapeDtypeStruct((width // HD * MAXLEN + META, HD), jnp.bfloat16)
    scratch = [pltpu.SMEM((sections,), jnp.int32), pltpu.SMEM((sections,), jnp.int32)]
    params = pltpu.CompilerParams(vmem_limit_bytes=VMEM_LIMIT)
    kv, *front = pl.pallas_call(
        functools.partial(pack_first_kernel, turns=turns),
        out_shape=[jax.ShapeDtypeStruct((rows, width), jnp.bfloat16)] + [block] * len(turns),
        in_specs=[SMEM, VMEM, VMEM, VMEM, SMEM, SMEM],
        out_specs=[VMEM] * (1 + len(turns)),
        scratch_shapes=scratch,
        compiler_params=params,
        name="pack_first",
    )(me, keep, recv, send, lengths, decode_host)
    others = [k for k in range(sections) if k not in turns]
    rest = pl.pallas_call(
        functools.partial(pack_rest_kernel, turns=others),
        out_shape=[block] * len(others),
        in_specs=[SMEM, VMEM, SMEM, SMEM],
        out_specs=[VMEM] * len(others),
        scratch_shapes=scratch,
        compiler_params=params,
        cost_estimate=pl.CostEstimate(flops=1 << 24, bytes_accessed=4 << 20, transcendentals=0),
        name="pack_rest",
    )(me, kv, lengths, decode_host)
    return dict(zip(list(turns) + others, list(front) + list(rest)))


def attend_blocks(blocks, count_ref, q_ref, score_ref, value_ref, acc_ref):
    groups = q_ref.shape[0] // QPK
    scale = HD ** (-0.5)
    flat = QPK * BMAX
    lane = lax.broadcasted_iota(jnp.int32, (flat, MAXLEN), 1)
    beam = lax.broadcasted_iota(jnp.int32, (QPK, BMAX, HD), 1)
    work = []
    for block in blocks:
        meta = block[2 * groups * MAXLEN :, :].astype(jnp.float32)
        slot = meta[0, 0].astype(jnp.int32)
        length = meta[0, 1].astype(jnp.int32)
        start = 0
        for i in range(count_ref.shape[1]):
            start = start + jnp.where(i < slot, count_ref[0, i], 0)
        for g in range(groups):
            work.append((block, g, length, pl.ds(start, BMAX), count_ref[0, slot]))
    scores = []
    for block, g, length, at, count in work:
        q = q_ref[g * QPK : (g + 1) * QPK, at, :].reshape(flat, HD).astype(jnp.bfloat16)
        keys = block[2 * g * MAXLEN : (2 * g + 1) * MAXLEN, :]
        raw = lax.dot_general(q, keys, (((1,), (1,)), ((), ())), preferred_element_type=jnp.float32)
        scores.append(jnp.where(lane < length, raw * scale, -jnp.inf))
    tops, owns = [], []
    for (block, g, length, at, count), score in zip(work, scores):
        own = score_ref[g * QPK : (g + 1) * QPK, at, :].reshape(flat, HD)[:, :1]
        owns.append(own)
        tops.append(jnp.maximum(jnp.max(score, axis=1, keepdims=True), own))
    expos = [jnp.exp(score - top) for score, top in zip(scores, tops)]
    own_expos = [jnp.exp(own - top) for own, top in zip(owns, tops)]
    totals = [jnp.sum(e, axis=1, keepdims=True) + o for e, o in zip(expos, own_expos)]
    weights = [(e / t).astype(jnp.bfloat16) for e, t in zip(expos, totals)]
    own_weights = [(o / t).astype(jnp.bfloat16).astype(jnp.float32) for o, t in zip(own_expos, totals)]
    mixes = []
    for (block, g, length, at, count), weight in zip(work, weights):
        values = block[(2 * g + 1) * MAXLEN : (2 * g + 2) * MAXLEN, :]
        mixes.append(jnp.dot(weight, values, preferred_element_type=jnp.float32))
    for (block, g, length, at, count), mix, own in zip(work, mixes, own_weights):
        own = own.reshape(QPK, BMAX, 1) * value_ref[g, at, :][None]
        heads = slice(g * QPK, (g + 1) * QPK)
        acc_ref[heads, at, :] = jnp.where(
            beam < count, mix.reshape(QPK, BMAX, HD) + own, acc_ref[heads, at, :]
        )


def first_kernel(query_ref, own_ref, count_ref, block_ref, q_ref, score_ref, value_ref, acc_ref):
    beams = query_ref.shape[0]
    heads = query_ref.shape[1] // HD
    scale = HD ** (-0.5)
    tail = jnp.zeros((BMAX, HD), jnp.float32)
    for g in range(heads // QPK):
        key = own_ref[:, 2 * g * HD : (2 * g + 1) * HD].astype(jnp.float32)
        value_ref[g, :beams, :] = own_ref[:, (2 * g + 1) * HD : (2 * g + 2) * HD].astype(jnp.float32)
        value_ref[g, beams:, :] = tail
        for h in range(g * QPK, (g + 1) * QPK):
            q = query_ref[:, h * HD : (h + 1) * HD].astype(jnp.float32)
            q_ref[h, :beams, :] = q
            q_ref[h, beams:, :] = tail
            score = jnp.sum(q * key, axis=1, keepdims=True) * scale
            score_ref[h, :beams, :] = jnp.broadcast_to(score, (beams, HD))
            score_ref[h, beams:, :] = tail
    acc_ref[...] = jnp.zeros_like(acc_ref)
    attend_blocks([block_ref], count_ref, q_ref, score_ref, value_ref, acc_ref)


def attend_first(query, own, counts, block):
    beams, width = query.shape
    heads = width // HD
    tall = jax.ShapeDtypeStruct((heads, beams + BMAX, HD), jnp.float32)
    return pl.pallas_call(
        first_kernel,
        out_shape=(tall, tall, jax.ShapeDtypeStruct((heads // QPK, beams + BMAX, HD), jnp.float32), tall),
        in_specs=[VMEM, VMEM, SMEM, VMEM],
        out_specs=(VMEM,) * 4,
        compiler_params=pltpu.CompilerParams(vmem_limit_bytes=VMEM_LIMIT),
        cost_estimate=pl.CostEstimate(flops=1 << 24, bytes_accessed=4 << 20, transcendentals=0),
        name="attend_first",
    )(query, own, counts, block)


def later_kernel(count_ref, q_ref, score_ref, value_ref, acc_in, *refs, n_blocks, last):
    blocks, rest = refs[:n_blocks], refs[n_blocks:]
    acc_ref = rest[0]
    for base in range(0, n_blocks, GROUP // 2):
        attend_blocks(blocks[base : base + GROUP // 2], count_ref, q_ref, score_ref, value_ref, acc_ref)
    if last:
        out_ref = rest[1]
        beams = out_ref.shape[0]
        for h in range(acc_ref.shape[0]):
            out_ref[:, h * HD : (h + 1) * HD] = acc_ref[h, :beams, :].astype(jnp.bfloat16)


def attend_later(counts, q, score, value, acc, blocks, out_shape):
    last = out_shape is not None
    shapes = [jax.ShapeDtypeStruct(acc.shape, acc.dtype)]
    if last:
        shapes.append(out_shape)
    return pl.pallas_call(
        functools.partial(later_kernel, n_blocks=len(blocks), last=last),
        out_shape=shapes,
        in_specs=[SMEM] + [VMEM] * (4 + len(blocks)),
        out_specs=[VMEM] * len(shapes),
        input_output_aliases={4: 0},
        compiler_params=pltpu.CompilerParams(vmem_limit_bytes=VMEM_LIMIT),
        cost_estimate=pl.CostEstimate(flops=1 << 24, bytes_accessed=4 << 20, transcendentals=0),
        name="attend_last" if last else "attend_more",
    )(counts, q, score, value, acc, *blocks)


def per_device(tokens, norm_gain, kv_weight, lengths, decode_host, beam_counts, beam_query, beam_newkv):
    sections = lax.axis_size("section")
    mine = lax.axis_index("tensor").astype(jnp.int32).reshape(1)
    me = lax.axis_index("section").astype(jnp.int32).reshape(1)
    gain = norm_gain.reshape(-1, HD)
    send, scaled = project_send(1 - mine, tokens, gain, kv_weight)
    recv = lax.ppermute(send, "tensor", [(0, 1), (1, 0)])
    keep = project_keep(mine, scaled, kv_weight)
    front = (sections - 1, sections - 2)
    blocks = pack(me, keep, recv, send, lengths, decode_host, sections, front)
    got = {}
    for k in range(1, sections):
        got[k] = lax.ppermute(blocks[k], "section", [(s, s ^ k) for s in range(sections)])
    q, score, value, acc = attend_first(beam_query, beam_newkv, beam_counts, blocks[0])
    order = ORDER if sections == len(ORDER) + 1 else tuple(range(sections - 1, 0, -1))
    for part in (order[:3], order[3:-1]):
        (acc,) = attend_later(beam_counts, q, score, value, acc, [got[k] for k in part], None)
    late = [got[order[-1]]]
    out_shape = jax.ShapeDtypeStruct(beam_query.shape, jnp.bfloat16)
    return attend_later(beam_counts, q, score, value, acc, late, out_shape)[1]


def solution(mesh):
    rows = ("groups", "section")
    placed = (
        P(rows, "tensor"),
        P("tensor"),
        P("tensor", None),
        P(rows, None),
        P(rows, None),
        P(rows, None),
        P(rows, "tensor"),
        P(rows, "tensor"),
    )
    return jax.shard_map(
        per_device,
        mesh=mesh,
        in_specs=placed,
        out_specs=P(rows, "tensor"),
        check_vma=False,
    )
```

```python
import functools

import jax
import jax.numpy as jnp
from jax import lax
from jax.experimental import pallas as pl
from jax.experimental.pallas import tpu as pltpu
from jax.sharding import PartitionSpec as P

D = 8192
QPK = 8
HD = 128
BMAX = 16
MAXLEN = 96
META = 8
STEP = 1024
GROUP = 8
ORDER = (7, 3, 6, 2, 5, 1, 4)
VMEM_LIMIT = 44 * 1024 * 1024
PROJECT_LIMIT = 52800000

VMEM = pl.BlockSpec(memory_space=pltpu.VMEM)
SMEM = pl.BlockSpec(memory_space=pltpu.SMEM)
HBM = pl.BlockSpec(memory_space=pltpu.HBM)


def weight_copy(w_ref, w_buf, sem, half, c):
    width = w_buf.shape[2]
    columns = pl.ds(pl.multiple_of(half * width, width), width)
    rows = pl.ds(pl.multiple_of(c * STEP, STEP), STEP)
    return pltpu.make_async_copy(w_ref.at[rows, columns], w_buf.at[c], sem.at[c])


def project_send_kernel(half_ref, tok_ref, gain_hbm, w_ref, out_ref, scaled_ref, gain_buf, gain_ref, tok_buf, w_buf, gain_sem, tok_sem, w_sem):
    half = half_ref[0]
    steps = w_buf.shape[0]
    width = w_buf.shape[2]
    blocks = STEP // HD

    def token_copy(c):
        columns = pl.ds(pl.multiple_of(c * STEP, STEP), STEP)
        return pltpu.make_async_copy(tok_ref.at[:, columns], tok_buf.at[c], tok_sem.at[c])

    def begin(c, _):
        token_copy(c).start()
        weight_copy(w_ref, w_buf, w_sem, half, c).start()
        return _

    def step(c, _):
        token_copy(c).wait()
        squares = out_ref[:, width:]
        for b in range(blocks):
            tok = tok_buf[c, :, b * HD : (b + 1) * HD].astype(jnp.float32)
            scale = gain_ref[pl.ds(c * blocks + b, 1), :]
            scaled_ref[c, :, b * HD : (b + 1) * HD] = (tok * scale).astype(jnp.bfloat16)
            squares = squares + tok * tok
        out_ref[:, width:] = squares
        weight_copy(w_ref, w_buf, w_sem, half, c).wait()
        out_ref[:, :width] += jnp.dot(scaled_ref[c], w_buf[c], preferred_element_type=jnp.float32)
        return _

    gain_copy = pltpu.make_async_copy(gain_hbm, gain_buf, gain_sem.at[0])
    gain_copy.start()
    out_ref[...] = jnp.zeros_like(out_ref)
    lax.fori_loop(0, steps, begin, 0)
    gain_copy.wait()
    gain_ref[...] = gain_buf[...].astype(jnp.float32)
    lax.fori_loop(0, steps, step, 0)


def project_keep_kernel(half_ref, scaled_ref, w_ref, out_ref, w_buf, w_sem):
    half = half_ref[0]
    steps = w_buf.shape[0]

    for c in range(steps):
        weight_copy(w_ref, w_buf, w_sem, half, c).start()
    for c in range(steps):
        weight_copy(w_ref, w_buf, w_sem, half, c).wait()
        part = jnp.dot(scaled_ref[c], w_buf[c], preferred_element_type=jnp.float32)
        if c == 0:
            out_ref[...] = part
        else:
            out_ref[...] += part


def project_cost(rows, depth, width):
    return pl.CostEstimate(
        flops=2 * rows * depth * width,
        bytes_accessed=2 * depth * (rows + width) + 4 * rows * width,
        transcendentals=0,
    )


def project_send(half, tokens, gain, weight):
    rows, depth = tokens.shape
    width = weight.shape[1] // 2
    steps = depth // STEP
    return pl.pallas_call(
        project_send_kernel,
        out_shape=(
            jax.ShapeDtypeStruct((rows, width + HD), jnp.float32),
            jax.ShapeDtypeStruct((steps, rows, STEP), jnp.bfloat16),
        ),
        in_specs=[SMEM, HBM, HBM, HBM],
        out_specs=(VMEM, VMEM),
        scratch_shapes=[
            pltpu.VMEM(gain.shape, jnp.bfloat16),
            pltpu.VMEM(gain.shape, jnp.float32),
            pltpu.VMEM((steps, rows, STEP), jnp.bfloat16),
            pltpu.VMEM((steps, STEP, width), jnp.bfloat16),
            pltpu.SemaphoreType.DMA((1,)),
            pltpu.SemaphoreType.DMA((steps,)),
            pltpu.SemaphoreType.DMA((steps,)),
        ],
        compiler_params=pltpu.CompilerParams(vmem_limit_bytes=PROJECT_LIMIT),
        cost_estimate=project_cost(rows, depth, width),
        name="project_send",
    )(half, tokens, gain, weight)


def project_keep(half, scaled, weight):
    steps, rows, _ = scaled.shape
    depth = steps * STEP
    width = weight.shape[1] // 2
    return pl.pallas_call(
        project_keep_kernel,
        out_shape=jax.ShapeDtypeStruct((rows, width), jnp.float32),
        in_specs=[SMEM, VMEM, HBM],
        out_specs=VMEM,
        scratch_shapes=[
            pltpu.VMEM((steps, STEP, width), jnp.bfloat16),
            pltpu.SemaphoreType.DMA((steps,)),
        ],
        compiler_params=pltpu.CompilerParams(vmem_limit_bytes=VMEM_LIMIT),
        cost_estimate=project_cost(rows, depth, width),
        name="project_keep",
    )(half, scaled, weight)


def pack_blocks(turns, kv, me, len_ref, host_ref, outs, slot_ref, start_ref):
    rows, width = kv.shape
    start = 0
    for i in range(len_ref.shape[1]):
        turn = host_ref[0, i] ^ me
        slot_ref[turn] = i
        start_ref[turn] = start
        start = start + len_ref[0, i]
    lane = lax.broadcasted_iota(jnp.int32, (META, HD), 1)
    row_at = lax.broadcasted_iota(jnp.int32, (MAXLEN, rows), 1)
    row_at = row_at - lax.broadcasted_iota(jnp.int32, (MAXLEN, rows), 0)
    for base in range(0, len(turns), GROUP):
        part = turns[base : base + GROUP]
        picks = [(row_at == start_ref[k]).astype(jnp.float32).astype(jnp.bfloat16) for k in part]
        blocks = jnp.dot(
            jnp.concatenate(picks, axis=0), kv, preferred_element_type=jnp.float32
        ).astype(jnp.bfloat16)
        for i, k in enumerate(part):
            out = outs[base + i]
            for g in range(width // HD):
                out[g * MAXLEN : (g + 1) * MAXLEN, :] = blocks[
                    i * MAXLEN : (i + 1) * MAXLEN, g * HD : (g + 1) * HD
                ]
            slot = slot_ref[k]
            meta = jnp.where(lane == 0, slot, jnp.where(lane == 1, len_ref[0, slot], 0))
            out[width // HD * MAXLEN :, :] = meta.astype(jnp.float32).astype(jnp.bfloat16)


def pack_first_kernel(me_ref, keep_ref, recv_ref, send_ref, len_ref, host_ref, kv_ref, *refs, turns):
    width = keep_ref.shape[1]
    squares = jnp.sum(recv_ref[:, width:] + send_ref[:, width:], axis=1, keepdims=True)
    inverse = lax.rsqrt(squares / D + 1e-05)
    kv = ((keep_ref[...] + recv_ref[:, :width]) * inverse).astype(jnp.bfloat16)
    kv_ref[...] = kv
    pack_blocks(turns, kv, me_ref[0], len_ref, host_ref, refs[:-2], refs[-2], refs[-1])


def pack_rest_kernel(me_ref, kv_ref, len_ref, host_ref, *refs, turns):
    pack_blocks(turns, kv_ref[...], me_ref[0], len_ref, host_ref, refs[:-2], refs[-2], refs[-1])


def pack(me, keep, recv, send, lengths, decode_host, sections, turns):
    rows, width = keep.shape
    block = jax.ShapeDtypeStruct((width // HD * MAXLEN + META, HD), jnp.bfloat16)
    scratch = [pltpu.SMEM((sections,), jnp.int32), pltpu.SMEM((sections,), jnp.int32)]
    params = pltpu.CompilerParams(vmem_limit_bytes=VMEM_LIMIT)
    kv, *front = pl.pallas_call(
        functools.partial(pack_first_kernel, turns=turns),
        out_shape=[jax.ShapeDtypeStruct((rows, width), jnp.bfloat16)] + [block] * len(turns),
        in_specs=[SMEM, VMEM, VMEM, VMEM, SMEM, SMEM],
        out_specs=[VMEM] * (1 + len(turns)),
        scratch_shapes=scratch,
        compiler_params=params,
        name="pack_first",
    )(me, keep, recv, send, lengths, decode_host)
    others = [k for k in range(sections) if k not in turns]
    rest = pl.pallas_call(
        functools.partial(pack_rest_kernel, turns=others),
        out_shape=[block] * len(others),
        in_specs=[SMEM, VMEM, SMEM, SMEM],
        out_specs=[VMEM] * len(others),
        scratch_shapes=scratch,
        compiler_params=params,
        cost_estimate=pl.CostEstimate(flops=1 << 24, bytes_accessed=4 << 20, transcendentals=0),
        name="pack_rest",
    )(me, kv, lengths, decode_host)
    return dict(zip(list(turns) + others, list(front) + list(rest)))


def attend_blocks(blocks, count_ref, q_ref, score_ref, value_ref, acc_ref):
    groups = q_ref.shape[0] // QPK
    scale = HD ** (-0.5)
    flat = QPK * BMAX
    lane = lax.broadcasted_iota(jnp.int32, (flat, MAXLEN), 1)
    beam = lax.broadcasted_iota(jnp.int32, (QPK, BMAX, HD), 1)
    work = []
    for block in blocks:
        meta = block[2 * groups * MAXLEN :, :].astype(jnp.float32)
        slot = meta[0, 0].astype(jnp.int32)
        length = meta[0, 1].astype(jnp.int32)
        start = 0
        for i in range(count_ref.shape[1]):
            start = start + jnp.where(i < slot, count_ref[0, i], 0)
        for g in range(groups):
            work.append((block, g, length, pl.ds(start, BMAX), count_ref[0, slot]))
    scores = []
    for block, g, length, at, count in work:
        q = q_ref[g * QPK : (g + 1) * QPK, at, :].reshape(flat, HD).astype(jnp.bfloat16)
        keys = block[2 * g * MAXLEN : (2 * g + 1) * MAXLEN, :]
        raw = lax.dot_general(q, keys, (((1,), (1,)), ((), ())), preferred_element_type=jnp.float32)
        scores.append(jnp.where(lane < length, raw * scale, -jnp.inf))
    tops, owns = [], []
    for (block, g, length, at, count), score in zip(work, scores):
        own = score_ref[g * QPK : (g + 1) * QPK, at, :].reshape(flat, HD)[:, :1]
        owns.append(own)
        tops.append(jnp.maximum(jnp.max(score, axis=1, keepdims=True), own))
    expos = [jnp.exp(score - top) for score, top in zip(scores, tops)]
    own_expos = [jnp.exp(own - top) for own, top in zip(owns, tops)]
    totals = [jnp.sum(e, axis=1, keepdims=True) + o for e, o in zip(expos, own_expos)]
    weights = [(e / t).astype(jnp.bfloat16) for e, t in zip(expos, totals)]
    own_weights = [(o / t).astype(jnp.bfloat16).astype(jnp.float32) for o, t in zip(own_expos, totals)]
    mixes = []
    for (block, g, length, at, count), weight in zip(work, weights):
        values = block[(2 * g + 1) * MAXLEN : (2 * g + 2) * MAXLEN, :]
        mixes.append(jnp.dot(weight, values, preferred_element_type=jnp.float32))
    for (block, g, length, at, count), mix, own in zip(work, mixes, own_weights):
        own = own.reshape(QPK, BMAX, 1) * value_ref[g, at, :][None]
        heads = slice(g * QPK, (g + 1) * QPK)
        acc_ref[heads, at, :] = jnp.where(
            beam < count, mix.reshape(QPK, BMAX, HD) + own, acc_ref[heads, at, :]
        )


def first_kernel(query_ref, own_ref, count_ref, block_ref, q_ref, score_ref, value_ref, acc_ref):
    beams = query_ref.shape[0]
    heads = query_ref.shape[1] // HD
    scale = HD ** (-0.5)
    tail = jnp.zeros((BMAX, HD), jnp.float32)
    for g in range(heads // QPK):
        key = own_ref[:, 2 * g * HD : (2 * g + 1) * HD].astype(jnp.float32)
        value_ref[g, :beams, :] = own_ref[:, (2 * g + 1) * HD : (2 * g + 2) * HD].astype(jnp.float32)
        value_ref[g, beams:, :] = tail
        for h in range(g * QPK, (g + 1) * QPK):
            q = query_ref[:, h * HD : (h + 1) * HD].astype(jnp.float32)
            q_ref[h, :beams, :] = q
            q_ref[h, beams:, :] = tail
            score = jnp.sum(q * key, axis=1, keepdims=True) * scale
            score_ref[h, :beams, :] = jnp.broadcast_to(score, (beams, HD))
            score_ref[h, beams:, :] = tail
    acc_ref[...] = jnp.zeros_like(acc_ref)
    attend_blocks([block_ref], count_ref, q_ref, score_ref, value_ref, acc_ref)


def attend_first(query, own, counts, block):
    beams, width = query.shape
    heads = width // HD
    tall = jax.ShapeDtypeStruct((heads, beams + BMAX, HD), jnp.float32)
    return pl.pallas_call(
        first_kernel,
        out_shape=(tall, tall, jax.ShapeDtypeStruct((heads // QPK, beams + BMAX, HD), jnp.float32), tall),
        in_specs=[VMEM, VMEM, SMEM, VMEM],
        out_specs=(VMEM,) * 4,
        compiler_params=pltpu.CompilerParams(vmem_limit_bytes=VMEM_LIMIT),
        cost_estimate=pl.CostEstimate(flops=1 << 24, bytes_accessed=4 << 20, transcendentals=0),
        name="attend_first",
    )(query, own, counts, block)


def later_kernel(count_ref, q_ref, score_ref, value_ref, acc_in, *refs, n_blocks, last):
    blocks, rest = refs[:n_blocks], refs[n_blocks:]
    acc_ref = rest[0]
    for base in range(0, n_blocks, GROUP // 2):
        attend_blocks(blocks[base : base + GROUP // 2], count_ref, q_ref, score_ref, value_ref, acc_ref)
    if last:
        out_ref = rest[1]
        beams = out_ref.shape[0]
        for h in range(acc_ref.shape[0]):
            out_ref[:, h * HD : (h + 1) * HD] = acc_ref[h, :beams, :].astype(jnp.bfloat16)


def attend_later(counts, q, score, value, acc, blocks, out_shape):
    last = out_shape is not None
    shapes = [jax.ShapeDtypeStruct(acc.shape, acc.dtype)]
    if last:
        shapes.append(out_shape)
    return pl.pallas_call(
        functools.partial(later_kernel, n_blocks=len(blocks), last=last),
        out_shape=shapes,
        in_specs=[SMEM] + [VMEM] * (4 + len(blocks)),
        out_specs=[VMEM] * len(shapes),
        input_output_aliases={4: 0},
        compiler_params=pltpu.CompilerParams(vmem_limit_bytes=VMEM_LIMIT),
        cost_estimate=pl.CostEstimate(flops=1 << 24, bytes_accessed=4 << 20, transcendentals=0),
        name="attend_last" if last else "attend_more",
    )(counts, q, score, value, acc, *blocks)


def per_device(tokens, norm_gain, kv_weight, lengths, decode_host, beam_counts, beam_query, beam_newkv):
    sections = lax.axis_size("section")
    mine = lax.axis_index("tensor").astype(jnp.int32).reshape(1)
    me = lax.axis_index("section").astype(jnp.int32).reshape(1)
    gain = pltpu.with_memory_space_constraint(norm_gain.reshape(-1, HD), pltpu.HBM)
    send, scaled = project_send(1 - mine, tokens, gain, kv_weight)
    recv = lax.ppermute(send, "tensor", [(0, 1), (1, 0)])
    keep = project_keep(mine, scaled, kv_weight)
    front = (sections - 1, sections - 2)
    blocks = pack(me, keep, recv, send, lengths, decode_host, sections, front)
    got = {}
    for k in range(1, sections):
        got[k] = lax.ppermute(blocks[k], "section", [(s, s ^ k) for s in range(sections)])
    q, score, value, acc = attend_first(beam_query, beam_newkv, beam_counts, blocks[0])
    order = ORDER if sections == len(ORDER) + 1 else tuple(range(sections - 1, 0, -1))
    for part in (order[:3], order[3:-1]):
        (acc,) = attend_later(beam_counts, q, score, value, acc, [got[k] for k in part], None)
    late = [got[order[-1]]]
    out_shape = jax.ShapeDtypeStruct(beam_query.shape, jnp.bfloat16)
    return attend_later(beam_counts, q, score, value, acc, late, out_shape)[1]


def solution(mesh):
    rows = ("groups", "section")
    placed = (
        P(rows, "tensor"),
        P("tensor"),
        P("tensor", None),
        P(rows, None),
        P(rows, None),
        P(rows, None),
        P(rows, "tensor"),
        P(rows, "tensor"),
    )
    return jax.shard_map(
        per_device,
        mesh=mesh,
        in_specs=placed,
        out_specs=P(rows, "tensor"),
        check_vma=False,
    )
```

```python
import functools

import jax
import jax.numpy as jnp
from jax import lax
from jax.experimental import pallas as pl
from jax.experimental.pallas import tpu as pltpu
from jax.sharding import PartitionSpec as P

D = 8192
QPK = 8
HD = 128
BMAX = 16
MAXLEN = 96
META = 8
STEP = 1024
GROUP = 8
FRONT = 2
ORDER = (7, 3, 6, 2, 5, 1, 4)
VMEM_LIMIT = 44 * 1024 * 1024
PROJECT_LIMIT = VMEM_LIMIT

VMEM = pl.BlockSpec(memory_space=pltpu.VMEM)
SMEM = pl.BlockSpec(memory_space=pltpu.SMEM)
HBM = pl.BlockSpec(memory_space=pltpu.HBM)


def weight_copy(w_ref, w_buf, sem, half, c):
    width = w_buf.shape[2]
    columns = pl.ds(pl.multiple_of(half * width, width), width)
    rows = pl.ds(pl.multiple_of(c * STEP, STEP), STEP)
    return pltpu.make_async_copy(w_ref.at[rows, columns], w_buf.at[c], sem.at[c])


def project_send_kernel(tok_ref, gain_hbm, w_ref, out_ref, scaled_ref, gain_buf, gain_ref, tok_buf, w_buf, gain_sem, tok_sem, w_sem):
    half = 1 - lax.axis_index("tensor")
    steps = w_buf.shape[0]
    width = w_buf.shape[2]
    blocks = STEP // HD

    def token_copy(c):
        columns = pl.ds(pl.multiple_of(c * STEP, STEP), STEP)
        return pltpu.make_async_copy(tok_ref.at[:, columns], tok_buf.at[c], tok_sem.at[c])

    def begin(c, _):
        token_copy(c).start()
        weight_copy(w_ref, w_buf, w_sem, half, c).start()
        return _

    def step(c, _):
        token_copy(c).wait()
        squares = out_ref[:, width:]
        for b in range(blocks):
            tok = tok_buf[c, :, b * HD : (b + 1) * HD].astype(jnp.float32)
            scale = gain_ref[pl.ds(c * blocks + b, 1), :]
            scaled_ref[c, :, b * HD : (b + 1) * HD] = (tok * scale).astype(jnp.bfloat16)
            squares = squares + tok * tok
        out_ref[:, width:] = squares
        weight_copy(w_ref, w_buf, w_sem, half, c).wait()
        out_ref[:, :width] += jnp.dot(scaled_ref[c], w_buf[c], preferred_element_type=jnp.float32)
        return _

    gain_copy = pltpu.make_async_copy(gain_hbm, gain_buf, gain_sem.at[0])
    gain_copy.start()
    out_ref[...] = jnp.zeros_like(out_ref)
    lax.fori_loop(0, steps, begin, 0)
    gain_copy.wait()
    gain_ref[...] = gain_buf[...].astype(jnp.float32)
    lax.fori_loop(0, steps, step, 0)


def make_picks(order, me, rows, len_ref, host_ref, pick_ref, meta_ref, slot_ref, start_ref):
    start = 0
    for i in range(len_ref.shape[1]):
        turn = host_ref[0, i] ^ me
        slot_ref[turn] = i
        start_ref[turn] = start
        start = start + len_ref[0, i]
    lane = lax.broadcasted_iota(jnp.int32, (META, HD), 1)
    row_at = lax.broadcasted_iota(jnp.int32, (MAXLEN, rows), 1)
    row_at = row_at - lax.broadcasted_iota(jnp.int32, (MAXLEN, rows), 0)
    for i, k in enumerate(order):
        hit = (row_at == start_ref[k]).astype(jnp.float32).astype(jnp.bfloat16)
        pick_ref[i * MAXLEN : (i + 1) * MAXLEN, :] = hit
        slot = slot_ref[k]
        meta = jnp.where(lane == 0, slot, jnp.where(lane == 1, len_ref[0, slot], 0))
        meta_ref[i] = meta.astype(jnp.float32)


def project_keep_kernel(len_hbm, host_hbm, scaled_ref, w_ref, out_ref, pick_ref, meta_ref, w_buf, w_sem, len_ref, host_ref, small_sem, slot_ref, start_ref, *, order):
    half = lax.axis_index("tensor")
    steps = w_buf.shape[0]
    len_copy = pltpu.make_async_copy(len_hbm, len_ref, small_sem.at[0])
    host_copy = pltpu.make_async_copy(host_hbm, host_ref, small_sem.at[1])
    len_copy.start()
    host_copy.start()
    for c in range(steps):
        weight_copy(w_ref, w_buf, w_sem, half, c).start()
    len_copy.wait()
    host_copy.wait()
    make_picks(order, lax.axis_index("section"), out_ref.shape[0], len_ref, host_ref, pick_ref, meta_ref, slot_ref, start_ref)
    for c in range(steps):
        weight_copy(w_ref, w_buf, w_sem, half, c).wait()
        part = jnp.dot(scaled_ref[c], w_buf[c], preferred_element_type=jnp.float32)
        if c == 0:
            out_ref[...] = part
        else:
            out_ref[...] += part


def project_cost(rows, depth, width):
    return pl.CostEstimate(
        flops=2 * rows * depth * width,
        bytes_accessed=2 * depth * (rows + width) + 4 * rows * width,
        transcendentals=0,
    )


def project_send(tokens, gain, weight):
    rows, depth = tokens.shape
    width = weight.shape[1] // 2
    steps = depth // STEP
    return pl.pallas_call(
        project_send_kernel,
        out_shape=(
            jax.ShapeDtypeStruct((rows, width + HD), jnp.float32),
            jax.ShapeDtypeStruct((steps, rows, STEP), jnp.bfloat16),
        ),
        in_specs=[HBM, HBM, HBM],
        out_specs=(VMEM, VMEM),
        scratch_shapes=[
            pltpu.VMEM(gain.shape, jnp.bfloat16),
            pltpu.VMEM(gain.shape, jnp.float32),
            pltpu.VMEM((steps, rows, STEP), jnp.bfloat16),
            pltpu.VMEM((steps, STEP, width), jnp.bfloat16),
            pltpu.SemaphoreType.DMA((1,)),
            pltpu.SemaphoreType.DMA((steps,)),
            pltpu.SemaphoreType.DMA((steps,)),
        ],
        compiler_params=pltpu.CompilerParams(vmem_limit_bytes=PROJECT_LIMIT),
        cost_estimate=project_cost(rows, depth, width),
        name="project_send",
    )(tokens, gain, weight)


def project_keep(lengths, decode_host, scaled, weight, order):
    steps, rows, _ = scaled.shape
    depth = steps * STEP
    width = weight.shape[1] // 2
    sections = len(order)
    return pl.pallas_call(
        functools.partial(project_keep_kernel, order=order),
        out_shape=(
            jax.ShapeDtypeStruct((rows, width), jnp.float32),
            jax.ShapeDtypeStruct((sections * MAXLEN, rows), jnp.bfloat16),
            jax.ShapeDtypeStruct((sections, META, HD), jnp.float32),
        ),
        in_specs=[HBM, HBM, VMEM, HBM],
        out_specs=(VMEM, VMEM, VMEM),
        scratch_shapes=[
            pltpu.VMEM((steps, STEP, width), jnp.bfloat16),
            pltpu.SemaphoreType.DMA((steps,)),
            pltpu.SMEM((1, sections), jnp.int32),
            pltpu.SMEM((1, sections), jnp.int32),
            pltpu.SemaphoreType.DMA((2,)),
            pltpu.SMEM((sections,), jnp.int32),
            pltpu.SMEM((sections,), jnp.int32),
        ],
        compiler_params=pltpu.CompilerParams(vmem_limit_bytes=VMEM_LIMIT),
        cost_estimate=project_cost(rows, depth, width),
        name="project_keep",
    )(lengths, decode_host, scaled, weight)


def pack_blocks(first, kv, pick_ref, meta_ref, outs):
    width = kv.shape[1]
    for base in range(0, len(outs), GROUP):
        part = outs[base : base + GROUP]
        top = (first + base) * MAXLEN
        picks = pick_ref[top : top + len(part) * MAXLEN, :]
        blocks = jnp.dot(picks, kv, preferred_element_type=jnp.float32).astype(jnp.bfloat16)
        for i, out in enumerate(part):
            for g in range(width // HD):
                out[g * MAXLEN : (g + 1) * MAXLEN, :] = blocks[
                    i * MAXLEN : (i + 1) * MAXLEN, g * HD : (g + 1) * HD
                ]
            out[width // HD * MAXLEN :, :] = meta_ref[first + base + i].astype(jnp.bfloat16)


def pack_kernel(keep_ref, recv_ref, send_ref, pick_ref, meta_ref, *outs):
    width = keep_ref.shape[1]
    squares = jnp.sum(recv_ref[:, width:] + send_ref[:, width:], axis=1, keepdims=True)
    inverse = lax.rsqrt(squares / D + 1e-05)
    kv = ((keep_ref[...] + recv_ref[:, :width]) * inverse).astype(jnp.bfloat16)
    pack_blocks(0, kv, pick_ref, meta_ref, outs)


def pack(keep, recv, send, picks, metas, order):
    rows, width = keep.shape
    block = jax.ShapeDtypeStruct((width // HD * MAXLEN + META, HD), jnp.bfloat16)
    blocks = pl.pallas_call(
        pack_kernel,
        out_shape=[block] * len(order),
        in_specs=[VMEM] * 5,
        out_specs=[VMEM] * len(order),
        compiler_params=pltpu.CompilerParams(vmem_limit_bytes=VMEM_LIMIT),
        name="pack",
    )(keep, recv, send, picks, metas)
    return dict(zip(order, blocks))


def attend_blocks(blocks, table_ref, q_ref, score_ref, value_ref, acc_ref):
    groups = q_ref.shape[0] // QPK
    scale = HD ** (-0.5)
    flat = QPK * BMAX
    lane = lax.broadcasted_iota(jnp.int32, (flat, MAXLEN), 1)
    beam = lax.broadcasted_iota(jnp.int32, (QPK, BMAX, HD), 1)
    place = lax.broadcasted_iota(jnp.int32, table_ref.shape, 0).astype(jnp.float32)
    work = []
    for block in blocks:
        meta = block[2 * groups * MAXLEN :, :].astype(jnp.float32)
        length = meta[:1, 1:2].astype(jnp.int32)
        entry = jnp.sum(jnp.where(place == meta[:1, :1], table_ref[...], 0.0), axis=0, keepdims=True)
        start = entry[0, 0].astype(jnp.int32)
        count = entry[:1, 1:2].astype(jnp.int32)
        for g in range(groups):
            work.append((block, g, length, pl.ds(start, BMAX), count))
    scores = []
    for block, g, length, at, count in work:
        q = q_ref[g * QPK : (g + 1) * QPK, at, :].reshape(flat, HD).astype(jnp.bfloat16)
        keys = block[2 * g * MAXLEN : (2 * g + 1) * MAXLEN, :]
        raw = lax.dot_general(q, keys, (((1,), (1,)), ((), ())), preferred_element_type=jnp.float32)
        scores.append(jnp.where(lane < length, raw * scale, -jnp.inf))
    tops, owns = [], []
    for (block, g, length, at, count), score in zip(work, scores):
        own = score_ref[g * QPK : (g + 1) * QPK, at, :].reshape(flat, HD)[:, :1]
        owns.append(own)
        tops.append(jnp.maximum(jnp.max(score, axis=1, keepdims=True), own))
    expos = [jnp.exp(score - top) for score, top in zip(scores, tops)]
    own_expos = [jnp.exp(own - top) for own, top in zip(owns, tops)]
    totals = [jnp.sum(e, axis=1, keepdims=True) + o for e, o in zip(expos, own_expos)]
    weights = [(e / t).astype(jnp.bfloat16) for e, t in zip(expos, totals)]
    own_weights = [(o / t).astype(jnp.bfloat16).astype(jnp.float32) for o, t in zip(own_expos, totals)]
    mixes = []
    for (block, g, length, at, count), weight in zip(work, weights):
        values = block[(2 * g + 1) * MAXLEN : (2 * g + 2) * MAXLEN, :]
        mixes.append(jnp.dot(weight, values, preferred_element_type=jnp.float32))
    for (block, g, length, at, count), mix, own in zip(work, mixes, own_weights):
        own = own.reshape(QPK, BMAX, 1) * value_ref[g, at, :][None]
        heads = slice(g * QPK, (g + 1) * QPK)
        acc_ref[heads, at, :] = jnp.where(
            beam < count, mix.reshape(QPK, BMAX, HD) + own, acc_ref[heads, at, :]
        )


def first_kernel(query_ref, own_ref, count_ref, block_ref, q_ref, score_ref, value_ref, table_ref, acc_ref):
    beams = query_ref.shape[0]
    heads = query_ref.shape[1] // HD
    scale = HD ** (-0.5)
    tail = jnp.zeros((BMAX, HD), jnp.float32)
    for g in range(heads // QPK):
        key = own_ref[:, 2 * g * HD : (2 * g + 1) * HD].astype(jnp.float32)
        value_ref[g, :beams, :] = own_ref[:, (2 * g + 1) * HD : (2 * g + 2) * HD].astype(jnp.float32)
        value_ref[g, beams:, :] = tail
        for h in range(g * QPK, (g + 1) * QPK):
            q = query_ref[:, h * HD : (h + 1) * HD].astype(jnp.float32)
            q_ref[h, :beams, :] = q
            q_ref[h, beams:, :] = tail
            score = jnp.sum(q * key, axis=1, keepdims=True) * scale
            score_ref[h, :beams, :] = jnp.broadcast_to(score, (beams, HD))
            score_ref[h, beams:, :] = tail
    lane = lax.broadcasted_iota(jnp.int32, (1, HD), 1)
    start = 0
    for i in range(count_ref.shape[1]):
        count = count_ref[0, i]
        row = jnp.where(lane == 0, start, jnp.where(lane == 1, count, 0))
        table_ref[i : i + 1, :] = row.astype(jnp.float32)
        start = start + count
    acc_ref[...] = jnp.zeros_like(acc_ref)
    attend_blocks([block_ref], table_ref, q_ref, score_ref, value_ref, acc_ref)


def attend_first(query, own, counts, block):
    beams, width = query.shape
    heads = width // HD
    tall = jax.ShapeDtypeStruct((heads, beams + BMAX, HD), jnp.float32)
    return pl.pallas_call(
        first_kernel,
        out_shape=(
            tall,
            tall,
            jax.ShapeDtypeStruct((heads // QPK, beams + BMAX, HD), jnp.float32),
            jax.ShapeDtypeStruct((counts.shape[1], HD), jnp.float32),
            tall,
        ),
        in_specs=[VMEM, VMEM, SMEM, VMEM],
        out_specs=(VMEM,) * 5,
        compiler_params=pltpu.CompilerParams(vmem_limit_bytes=VMEM_LIMIT),
        cost_estimate=pl.CostEstimate(flops=1 << 24, bytes_accessed=4 << 20, transcendentals=0),
        name="attend_first",
    )(query, own, counts, block)


def later_kernel(table_ref, q_ref, score_ref, value_ref, acc_in, *refs, n_blocks, last):
    blocks, rest = refs[:n_blocks], refs[n_blocks:]
    acc_ref = rest[0]
    for base in range(0, n_blocks, GROUP // 2):
        attend_blocks(blocks[base : base + GROUP // 2], table_ref, q_ref, score_ref, value_ref, acc_ref)
    if last:
        out_ref = rest[1]
        beams = out_ref.shape[0]
        for h in range(acc_ref.shape[0]):
            out_ref[:, h * HD : (h + 1) * HD] = acc_ref[h, :beams, :].astype(jnp.bfloat16)


def attend_later(table, q, score, value, acc, blocks, out_shape):
    last = out_shape is not None
    shapes = [jax.ShapeDtypeStruct(acc.shape, acc.dtype)]
    if last:
        shapes.append(out_shape)
    return pl.pallas_call(
        functools.partial(later_kernel, n_blocks=len(blocks), last=last),
        out_shape=shapes,
        in_specs=[VMEM] * (5 + len(blocks)),
        out_specs=[VMEM] * len(shapes),
        input_output_aliases={4: 0},
        compiler_params=pltpu.CompilerParams(vmem_limit_bytes=VMEM_LIMIT),
        cost_estimate=pl.CostEstimate(flops=1 << 24, bytes_accessed=4 << 20, transcendentals=0),
        name="attend_last" if last else "attend_more",
    )(table, q, score, value, acc, *blocks)


def per_device(tokens, norm_gain, kv_weight, lengths, decode_host, beam_counts, beam_query, beam_newkv):
    sections = lax.axis_size("section")
    gain = pltpu.with_memory_space_constraint(norm_gain.reshape(-1, HD), pltpu.HBM)
    tokens = pltpu.with_memory_space_constraint(tokens, pltpu.HBM)
    send, scaled = project_send(tokens, gain, kv_weight)
    recv = lax.ppermute(send, "tensor", [(0, 1), (1, 0)])
    turns = tuple(range(sections - 1, -1, -1))
    keep, picks, metas = project_keep(lengths, decode_host, scaled, kv_weight, turns)
    blocks = pack(keep, recv, send, picks, metas, turns)
    got = {}
    for k in range(1, sections):
        got[k] = lax.ppermute(blocks[k], "section", [(s, s ^ k) for s in range(sections)])
    q, score, value, table, acc = attend_first(beam_query, beam_newkv, beam_counts, blocks[0])
    order = ORDER if sections == len(ORDER) + 1 else tuple(range(sections - 1, 0, -1))
    for part in (order[:3], order[3:-1]):
        (acc,) = attend_later(table, q, score, value, acc, [got[k] for k in part], None)
    late = [got[order[-1]]]
    out_shape = jax.ShapeDtypeStruct(beam_query.shape, jnp.bfloat16)
    return attend_later(table, q, score, value, acc, late, out_shape)[1]


def solution(mesh):
    rows = ("groups", "section")
    placed = (
        P(rows, "tensor"),
        P("tensor"),
        P("tensor", None),
        P(rows, None),
        P(rows, None),
        P(rows, None),
        P(rows, "tensor"),
        P(rows, "tensor"),
    )
    return jax.shard_map(
        per_device,
        mesh=mesh,
        in_specs=placed,
        out_specs=P(rows, "tensor"),
        check_vma=False,
    )
```

```python
import functools

import jax
import jax.numpy as jnp
from jax import lax
from jax.experimental import pallas as pl
from jax.experimental.pallas import tpu as pltpu
from jax.sharding import PartitionSpec as P

D = 8192
QPK = 8
HD = 128
BMAX = 16
MAXLEN = 96
META = 8
STEP = 1024
GROUP = 8
FRONT = 2
ORDER = (4, 2, 5, 3, 7, 1, 6)
VMEM_LIMIT = 44 * 1024 * 1024
PROJECT_LIMIT = VMEM_LIMIT

VMEM = pl.BlockSpec(memory_space=pltpu.VMEM)
SMEM = pl.BlockSpec(memory_space=pltpu.SMEM)
HBM = pl.BlockSpec(memory_space=pltpu.HBM)


def weight_copy(w_ref, w_buf, sem, half, c):
    width = w_buf.shape[2]
    columns = pl.ds(pl.multiple_of(half * width, width), width)
    rows = pl.ds(pl.multiple_of(c * STEP, STEP), STEP)
    return pltpu.make_async_copy(w_ref.at[rows, columns], w_buf.at[c], sem.at[c])


def project_send_kernel(tok_ref, gain_hbm, w_ref, out_ref, scaled_ref, gain_buf, gain_ref, tok_buf, w_buf, gain_sem, tok_sem, w_sem):
    half = 1 - lax.axis_index("tensor")
    steps = w_buf.shape[0]
    width = w_buf.shape[2]
    blocks = STEP // HD

    def token_copy(c):
        columns = pl.ds(pl.multiple_of(c * STEP, STEP), STEP)
        return pltpu.make_async_copy(tok_ref.at[:, columns], tok_buf.at[c], tok_sem.at[c])

    def begin(c, _):
        token_copy(c).start()
        weight_copy(w_ref, w_buf, w_sem, half, c).start()
        return _

    def step(c, _):
        token_copy(c).wait()
        squares = out_ref[:, width:]
        for b in range(blocks):
            tok = tok_buf[c, :, b * HD : (b + 1) * HD].astype(jnp.float32)
            scale = gain_ref[pl.ds(c * blocks + b, 1), :]
            scaled_ref[c, :, b * HD : (b + 1) * HD] = (tok * scale).astype(jnp.bfloat16)
            squares = squares + tok * tok
        out_ref[:, width:] = squares
        weight_copy(w_ref, w_buf, w_sem, half, c).wait()
        out_ref[:, :width] += jnp.dot(scaled_ref[c], w_buf[c], preferred_element_type=jnp.float32)
        return _

    gain_copy = pltpu.make_async_copy(gain_hbm, gain_buf, gain_sem.at[0])
    gain_copy.start()
    out_ref[...] = jnp.zeros_like(out_ref)
    lax.fori_loop(0, steps, begin, 0)
    gain_copy.wait()
    gain_ref[...] = gain_buf[...].astype(jnp.float32)
    lax.fori_loop(0, steps, step, 0)


def make_picks(order, me, rows, len_ref, host_ref, pick_ref, meta_ref, slot_ref, start_ref):
    start = 0
    for i in range(len_ref.shape[1]):
        turn = host_ref[0, i] ^ me
        slot_ref[turn] = i
        start_ref[turn] = start
        start = start + len_ref[0, i]
    lane = lax.broadcasted_iota(jnp.int32, (META, HD), 1)
    row_at = lax.broadcasted_iota(jnp.int32, (MAXLEN, rows), 1)
    row_at = row_at - lax.broadcasted_iota(jnp.int32, (MAXLEN, rows), 0)
    for i, k in enumerate(order):
        hit = (row_at == start_ref[k]).astype(jnp.float32).astype(jnp.bfloat16)
        pick_ref[i * MAXLEN : (i + 1) * MAXLEN, :] = hit
        slot = slot_ref[k]
        meta = jnp.where(lane == 0, slot, jnp.where(lane == 1, len_ref[0, slot], 0))
        meta_ref[i] = meta.astype(jnp.float32)


def project_keep_kernel(len_hbm, host_hbm, scaled_ref, w_ref, out_ref, pick_ref, meta_ref, w_buf, w_sem, len_ref, host_ref, small_sem, slot_ref, start_ref, *, order):
    half = lax.axis_index("tensor")
    steps = w_buf.shape[0]
    len_copy = pltpu.make_async_copy(len_hbm, len_ref, small_sem.at[0])
    host_copy = pltpu.make_async_copy(host_hbm, host_ref, small_sem.at[1])
    len_copy.start()
    host_copy.start()
    for c in range(steps):
        weight_copy(w_ref, w_buf, w_sem, half, c).start()
    len_copy.wait()
    host_copy.wait()
    make_picks(order, lax.axis_index("section"), out_ref.shape[0], len_ref, host_ref, pick_ref, meta_ref, slot_ref, start_ref)
    for c in range(steps):
        weight_copy(w_ref, w_buf, w_sem, half, c).wait()
        part = jnp.dot(scaled_ref[c], w_buf[c], preferred_element_type=jnp.float32)
        if c == 0:
            out_ref[...] = part
        else:
            out_ref[...] += part


def project_cost(rows, depth, width):
    return pl.CostEstimate(
        flops=2 * rows * depth * width,
        bytes_accessed=2 * depth * (rows + width) + 4 * rows * width,
        transcendentals=0,
    )


def project_send(tokens, gain, weight):
    rows, depth = tokens.shape
    width = weight.shape[1] // 2
    steps = depth // STEP
    return pl.pallas_call(
        project_send_kernel,
        out_shape=(
            jax.ShapeDtypeStruct((rows, width + HD), jnp.float32),
            jax.ShapeDtypeStruct((steps, rows, STEP), jnp.bfloat16),
        ),
        in_specs=[HBM, HBM, HBM],
        out_specs=(VMEM, VMEM),
        scratch_shapes=[
            pltpu.VMEM(gain.shape, jnp.bfloat16),
            pltpu.VMEM(gain.shape, jnp.float32),
            pltpu.VMEM((steps, rows, STEP), jnp.bfloat16),
            pltpu.VMEM((steps, STEP, width), jnp.bfloat16),
            pltpu.SemaphoreType.DMA((1,)),
            pltpu.SemaphoreType.DMA((steps,)),
            pltpu.SemaphoreType.DMA((steps,)),
        ],
        compiler_params=pltpu.CompilerParams(vmem_limit_bytes=PROJECT_LIMIT),
        cost_estimate=project_cost(rows, depth, width),
        name="project_send",
    )(tokens, gain, weight)


def project_keep(lengths, decode_host, scaled, weight, order):
    steps, rows, _ = scaled.shape
    depth = steps * STEP
    width = weight.shape[1] // 2
    sections = len(order)
    return pl.pallas_call(
        functools.partial(project_keep_kernel, order=order),
        out_shape=(
            jax.ShapeDtypeStruct((rows, width), jnp.float32),
            jax.ShapeDtypeStruct((sections * MAXLEN, rows), jnp.bfloat16),
            jax.ShapeDtypeStruct((sections, META, HD), jnp.float32),
        ),
        in_specs=[HBM, HBM, VMEM, HBM],
        out_specs=(VMEM, VMEM, VMEM),
        scratch_shapes=[
            pltpu.VMEM((steps, STEP, width), jnp.bfloat16),
            pltpu.SemaphoreType.DMA((steps,)),
            pltpu.SMEM((1, sections), jnp.int32),
            pltpu.SMEM((1, sections), jnp.int32),
            pltpu.SemaphoreType.DMA((2,)),
            pltpu.SMEM((sections,), jnp.int32),
            pltpu.SMEM((sections,), jnp.int32),
        ],
        compiler_params=pltpu.CompilerParams(vmem_limit_bytes=VMEM_LIMIT),
        cost_estimate=project_cost(rows, depth, width),
        name="project_keep",
    )(lengths, decode_host, scaled, weight)


def pack_blocks(first, kv, pick_ref, meta_ref, outs):
    width = kv.shape[1]
    for base in range(0, len(outs), GROUP):
        part = outs[base : base + GROUP]
        top = (first + base) * MAXLEN
        picks = pick_ref[top : top + len(part) * MAXLEN, :]
        blocks = jnp.dot(picks, kv, preferred_element_type=jnp.float32).astype(jnp.bfloat16)
        for i, out in enumerate(part):
            for g in range(width // HD):
                out[g * MAXLEN : (g + 1) * MAXLEN, :] = blocks[
                    i * MAXLEN : (i + 1) * MAXLEN, g * HD : (g + 1) * HD
                ]
            out[width // HD * MAXLEN :, :] = meta_ref[first + base + i].astype(jnp.bfloat16)


def pack_kernel(keep_ref, recv_ref, send_ref, pick_ref, meta_ref, *outs):
    width = keep_ref.shape[1]
    squares = jnp.sum(recv_ref[:, width:] + send_ref[:, width:], axis=1, keepdims=True)
    inverse = lax.rsqrt(squares / D + 1e-05)
    kv = ((keep_ref[...] + recv_ref[:, :width]) * inverse).astype(jnp.bfloat16)
    pack_blocks(0, kv, pick_ref, meta_ref, outs)


def pack(keep, recv, send, picks, metas, order):
    rows, width = keep.shape
    block = jax.ShapeDtypeStruct((width // HD * MAXLEN + META, HD), jnp.bfloat16)
    blocks = pl.pallas_call(
        pack_kernel,
        out_shape=[block] * len(order),
        in_specs=[VMEM] * 5,
        out_specs=[VMEM] * len(order),
        compiler_params=pltpu.CompilerParams(vmem_limit_bytes=VMEM_LIMIT),
        name="pack",
    )(keep, recv, send, picks, metas)
    return dict(zip(order, blocks))


def attend_blocks(blocks, table_ref, q_ref, score_ref, value_ref, acc_ref):
    groups = q_ref.shape[0] // QPK
    scale = HD ** (-0.5)
    flat = QPK * BMAX
    lane = lax.broadcasted_iota(jnp.int32, (flat, MAXLEN), 1)
    beam = lax.broadcasted_iota(jnp.int32, (QPK, BMAX, HD), 1)
    place = lax.broadcasted_iota(jnp.int32, table_ref.shape, 0).astype(jnp.float32)
    work = []
    for block in blocks:
        meta = block[2 * groups * MAXLEN :, :].astype(jnp.float32)
        length = meta[:1, 1:2].astype(jnp.int32)
        entry = jnp.sum(jnp.where(place == meta[:1, :1], table_ref[...], 0.0), axis=0, keepdims=True)
        start = entry[0, 0].astype(jnp.int32)
        count = entry[:1, 1:2].astype(jnp.int32)
        for g in range(groups):
            work.append((block, g, length, pl.ds(start, BMAX), count))
    scores = []
    for block, g, length, at, count in work:
        q = q_ref[g * QPK : (g + 1) * QPK, at, :].reshape(flat, HD).astype(jnp.bfloat16)
        keys = block[2 * g * MAXLEN : (2 * g + 1) * MAXLEN, :]
        raw = lax.dot_general(q, keys, (((1,), (1,)), ((), ())), preferred_element_type=jnp.float32)
        scores.append(jnp.where(lane < length, raw * scale, -jnp.inf))
    tops, owns = [], []
    for (block, g, length, at, count), score in zip(work, scores):
        own = score_ref[g * QPK : (g + 1) * QPK, at, :].reshape(flat, HD)[:, :1]
        owns.append(own)
        tops.append(jnp.maximum(jnp.max(score, axis=1, keepdims=True), own))
    expos = [jnp.exp(score - top) for score, top in zip(scores, tops)]
    own_expos = [jnp.exp(own - top) for own, top in zip(owns, tops)]
    totals = [jnp.sum(e, axis=1, keepdims=True) + o for e, o in zip(expos, own_expos)]
    weights = [(e / t).astype(jnp.bfloat16) for e, t in zip(expos, totals)]
    own_weights = [(o / t).astype(jnp.bfloat16).astype(jnp.float32) for o, t in zip(own_expos, totals)]
    mixes = []
    for (block, g, length, at, count), weight in zip(work, weights):
        values = block[(2 * g + 1) * MAXLEN : (2 * g + 2) * MAXLEN, :]
        mixes.append(jnp.dot(weight, values, preferred_element_type=jnp.float32))
    for (block, g, length, at, count), mix, own in zip(work, mixes, own_weights):
        own = own.reshape(QPK, BMAX, 1) * value_ref[g, at, :][None]
        heads = slice(g * QPK, (g + 1) * QPK)
        acc_ref[heads, at, :] = jnp.where(
            beam < count, mix.reshape(QPK, BMAX, HD) + own, acc_ref[heads, at, :]
        )


def first_kernel(query_ref, own_ref, count_ref, block_ref, q_ref, score_ref, value_ref, table_ref, acc_ref):
    beams = query_ref.shape[0]
    heads = query_ref.shape[1] // HD
    scale = HD ** (-0.5)
    tail = jnp.zeros((BMAX, HD), jnp.float32)
    for g in range(heads // QPK):
        key = own_ref[:, 2 * g * HD : (2 * g + 1) * HD].astype(jnp.float32)
        value_ref[g, :beams, :] = own_ref[:, (2 * g + 1) * HD : (2 * g + 2) * HD].astype(jnp.float32)
        value_ref[g, beams:, :] = tail
        for h in range(g * QPK, (g + 1) * QPK):
            q = query_ref[:, h * HD : (h + 1) * HD].astype(jnp.float32)
            q_ref[h, :beams, :] = q
            q_ref[h, beams:, :] = tail
            score = jnp.sum(q * key, axis=1, keepdims=True) * scale
            score_ref[h, :beams, :] = jnp.broadcast_to(score, (beams, HD))
            score_ref[h, beams:, :] = tail
    lane = lax.broadcasted_iota(jnp.int32, (1, HD), 1)
    start = 0
    for i in range(count_ref.shape[1]):
        count = count_ref[0, i]
        row = jnp.where(lane == 0, start, jnp.where(lane == 1, count, 0))
        table_ref[i : i + 1, :] = row.astype(jnp.float32)
        start = start + count
    acc_ref[...] = jnp.zeros_like(acc_ref)
    attend_blocks([block_ref], table_ref, q_ref, score_ref, value_ref, acc_ref)


def attend_first(query, own, counts, block):
    beams, width = query.shape
    heads = width // HD
    tall = jax.ShapeDtypeStruct((heads, beams + BMAX, HD), jnp.float32)
    return pl.pallas_call(
        first_kernel,
        out_shape=(
            tall,
            tall,
            jax.ShapeDtypeStruct((heads // QPK, beams + BMAX, HD), jnp.float32),
            jax.ShapeDtypeStruct((counts.shape[1], HD), jnp.float32),
            tall,
        ),
        in_specs=[VMEM, VMEM, SMEM, VMEM],
        out_specs=(VMEM,) * 5,
        compiler_params=pltpu.CompilerParams(vmem_limit_bytes=VMEM_LIMIT),
        cost_estimate=pl.CostEstimate(flops=1 << 24, bytes_accessed=4 << 20, transcendentals=0),
        name="attend_first",
    )(query, own, counts, block)


def later_kernel(table_ref, q_ref, score_ref, value_ref, acc_in, *refs, n_blocks, last):
    blocks, rest = refs[:n_blocks], refs[n_blocks:]
    acc_ref = rest[0]
    for base in range(0, n_blocks, GROUP // 2):
        attend_blocks(blocks[base : base + GROUP // 2], table_ref, q_ref, score_ref, value_ref, acc_ref)
    if last:
        out_ref = rest[1]
        beams = out_ref.shape[0]
        for h in range(acc_ref.shape[0]):
            out_ref[:, h * HD : (h + 1) * HD] = acc_ref[h, :beams, :].astype(jnp.bfloat16)


def attend_later(table, q, score, value, acc, blocks, out_shape):
    last = out_shape is not None
    shapes = [jax.ShapeDtypeStruct(acc.shape, acc.dtype)]
    if last:
        shapes.append(out_shape)
    return pl.pallas_call(
        functools.partial(later_kernel, n_blocks=len(blocks), last=last),
        out_shape=shapes,
        in_specs=[VMEM] * (5 + len(blocks)),
        out_specs=[VMEM] * len(shapes),
        input_output_aliases={4: 0},
        compiler_params=pltpu.CompilerParams(vmem_limit_bytes=VMEM_LIMIT),
        cost_estimate=pl.CostEstimate(flops=1 << 24, bytes_accessed=4 << 20, transcendentals=0),
        name="attend_last" if last else "attend_more",
    )(table, q, score, value, acc, *blocks)


def per_device(tokens, norm_gain, kv_weight, lengths, decode_host, beam_counts, beam_query, beam_newkv):
    sections = lax.axis_size("section")
    gain = pltpu.with_memory_space_constraint(norm_gain.reshape(-1, HD), pltpu.HBM)
    tokens = pltpu.with_memory_space_constraint(tokens, pltpu.HBM)
    send, scaled = project_send(tokens, gain, kv_weight)
    recv = lax.ppermute(send, "tensor", [(0, 1), (1, 0)])
    turns = tuple(range(sections - 1, -1, -1))
    keep, picks, metas = project_keep(lengths, decode_host, scaled, kv_weight, turns)
    blocks = pack(keep, recv, send, picks, metas, turns)
    got = {}
    for k in range(1, sections):
        got[k] = lax.ppermute(blocks[k], "section", [(s, s ^ k) for s in range(sections)])
    q, score, value, table, acc = attend_first(beam_query, beam_newkv, beam_counts, blocks[0])
    order = ORDER if sections == len(ORDER) + 1 else tuple(range(sections - 1, 0, -1))
    for part in (order[:3], order[3:-1]):
        (acc,) = attend_later(table, q, score, value, acc, [got[k] for k in part], None)
    late = [got[order[-1]]]
    out_shape = jax.ShapeDtypeStruct(beam_query.shape, jnp.bfloat16)
    return attend_later(table, q, score, value, acc, late, out_shape)[1]


def solution(mesh):
    rows = ("groups", "section")
    placed = (
        P(rows, "tensor"),
        P("tensor"),
        P("tensor", None),
        P(rows, None),
        P(rows, None),
        P(rows, None),
        P(rows, "tensor"),
        P(rows, "tensor"),
    )
    return jax.shard_map(
        per_device,
        mesh=mesh,
        in_specs=placed,
        out_specs=P(rows, "tensor"),
        check_vma=False,
    )
```

```python
import functools

import jax
import jax.numpy as jnp
from jax import lax
from jax.experimental import pallas as pl
from jax.experimental.pallas import tpu as pltpu
from jax.sharding import PartitionSpec as P

D = 8192
QPK = 8
HD = 128
BMAX = 16
MAXLEN = 96
META = 8
STEP = 512
GROUP = 8
FRONT = 2
ORDER = (4, 2, 5, 3, 7, 1, 6)
VMEM_LIMIT = 44 * 1024 * 1024
PROJECT_LIMIT = VMEM_LIMIT

VMEM = pl.BlockSpec(memory_space=pltpu.VMEM)
SMEM = pl.BlockSpec(memory_space=pltpu.SMEM)
HBM = pl.BlockSpec(memory_space=pltpu.HBM)


def weight_copy(w_ref, w_buf, sem, half, c):
    width = w_buf.shape[2]
    columns = pl.ds(pl.multiple_of(half * width, width), width)
    rows = pl.ds(pl.multiple_of(c * STEP, STEP), STEP)
    return pltpu.make_async_copy(w_ref.at[rows, columns], w_buf.at[c], sem.at[c])


def project_send_kernel(tok_ref, gain_hbm, w_ref, out_ref, scaled_ref, gain_buf, gain_ref, tok_buf, w_buf, gain_sem, tok_sem, w_sem):
    half = 1 - lax.axis_index("tensor")
    steps = w_buf.shape[0]
    width = w_buf.shape[2]
    blocks = STEP // HD

    def token_copy(c):
        columns = pl.ds(pl.multiple_of(c * STEP, STEP), STEP)
        return pltpu.make_async_copy(tok_ref.at[:, columns], tok_buf.at[c], tok_sem.at[c])

    def begin(c, _):
        token_copy(c).start()
        weight_copy(w_ref, w_buf, w_sem, half, c).start()
        return _

    def step(c, _):
        token_copy(c).wait()
        squares = out_ref[:, width:]
        for b in range(blocks):
            tok = tok_buf[c, :, b * HD : (b + 1) * HD].astype(jnp.float32)
            scale = gain_ref[pl.ds(c * blocks + b, 1), :]
            scaled_ref[c, :, b * HD : (b + 1) * HD] = (tok * scale).astype(jnp.bfloat16)
            squares = squares + tok * tok
        out_ref[:, width:] = squares
        weight_copy(w_ref, w_buf, w_sem, half, c).wait()
        out_ref[:, :width] += jnp.dot(scaled_ref[c], w_buf[c], preferred_element_type=jnp.float32)
        return _

    gain_copy = pltpu.make_async_copy(gain_hbm, gain_buf, gain_sem.at[0])
    gain_copy.start()
    out_ref[...] = jnp.zeros_like(out_ref)
    lax.fori_loop(0, steps, begin, 0)
    gain_copy.wait()
    gain_ref[...] = gain_buf[...].astype(jnp.float32)
    lax.fori_loop(0, steps, step, 0, unroll=2)


def make_picks(order, me, rows, len_ref, host_ref, pick_ref, meta_ref, slot_ref, start_ref):
    start = 0
    for i in range(len_ref.shape[1]):
        turn = host_ref[0, i] ^ me
        slot_ref[turn] = i
        start_ref[turn] = start
        start = start + len_ref[0, i]
    lane = lax.broadcasted_iota(jnp.int32, (META, HD), 1)
    row_at = lax.broadcasted_iota(jnp.int32, (MAXLEN, rows), 1)
    row_at = row_at - lax.broadcasted_iota(jnp.int32, (MAXLEN, rows), 0)
    for i, k in enumerate(order):
        hit = (row_at == start_ref[k]).astype(jnp.float32).astype(jnp.bfloat16)
        pick_ref[i * MAXLEN : (i + 1) * MAXLEN, :] = hit
        slot = slot_ref[k]
        meta = jnp.where(lane == 0, slot, jnp.where(lane == 1, len_ref[0, slot], 0))
        meta_ref[i] = meta.astype(jnp.float32)


def project_keep_kernel(len_hbm, host_hbm, scaled_ref, w_ref, out_ref, pick_ref, meta_ref, w_buf, w_sem, len_ref, host_ref, small_sem, slot_ref, start_ref, *, order):
    half = lax.axis_index("tensor")
    steps = w_buf.shape[0]
    len_copy = pltpu.make_async_copy(len_hbm, len_ref, small_sem.at[0])
    host_copy = pltpu.make_async_copy(host_hbm, host_ref, small_sem.at[1])
    len_copy.start()
    host_copy.start()
    for c in range(steps):
        weight_copy(w_ref, w_buf, w_sem, half, c).start()
    len_copy.wait()
    host_copy.wait()
    make_picks(order, lax.axis_index("section"), out_ref.shape[0], len_ref, host_ref, pick_ref, meta_ref, slot_ref, start_ref)
    for c in range(steps):
        weight_copy(w_ref, w_buf, w_sem, half, c).wait()
        part = jnp.dot(scaled_ref[c], w_buf[c], preferred_element_type=jnp.float32)
        if c == 0:
            out_ref[...] = part
        else:
            out_ref[...] += part


def project_cost(rows, depth, width):
    return pl.CostEstimate(
        flops=2 * rows * depth * width,
        bytes_accessed=2 * depth * (rows + width) + 4 * rows * width,
        transcendentals=0,
    )


def project_send(tokens, gain, weight):
    rows, depth = tokens.shape
    width = weight.shape[1] // 2
    steps = depth // STEP
    return pl.pallas_call(
        project_send_kernel,
        out_shape=(
            jax.ShapeDtypeStruct((rows, width + HD), jnp.float32),
            jax.ShapeDtypeStruct((steps, rows, STEP), jnp.bfloat16),
        ),
        in_specs=[HBM, HBM, HBM],
        out_specs=(VMEM, VMEM),
        scratch_shapes=[
            pltpu.VMEM(gain.shape, jnp.bfloat16),
            pltpu.VMEM(gain.shape, jnp.float32),
            pltpu.VMEM((steps, rows, STEP), jnp.bfloat16),
            pltpu.VMEM((steps, STEP, width), jnp.bfloat16),
            pltpu.SemaphoreType.DMA((1,)),
            pltpu.SemaphoreType.DMA((steps,)),
            pltpu.SemaphoreType.DMA((steps,)),
        ],
        compiler_params=pltpu.CompilerParams(vmem_limit_bytes=PROJECT_LIMIT),
        cost_estimate=project_cost(rows, depth, width),
        name="project_send",
    )(tokens, gain, weight)


def project_keep(lengths, decode_host, scaled, weight, order):
    steps, rows, _ = scaled.shape
    depth = steps * STEP
    width = weight.shape[1] // 2
    sections = len(order)
    return pl.pallas_call(
        functools.partial(project_keep_kernel, order=order),
        out_shape=(
            jax.ShapeDtypeStruct((rows, width), jnp.float32),
            jax.ShapeDtypeStruct((sections * MAXLEN, rows), jnp.bfloat16),
            jax.ShapeDtypeStruct((sections, META, HD), jnp.float32),
        ),
        in_specs=[HBM, HBM, VMEM, HBM],
        out_specs=(VMEM, VMEM, VMEM),
        scratch_shapes=[
            pltpu.VMEM((steps, STEP, width), jnp.bfloat16),
            pltpu.SemaphoreType.DMA((steps,)),
            pltpu.SMEM((1, sections), jnp.int32),
            pltpu.SMEM((1, sections), jnp.int32),
            pltpu.SemaphoreType.DMA((2,)),
            pltpu.SMEM((sections,), jnp.int32),
            pltpu.SMEM((sections,), jnp.int32),
        ],
        compiler_params=pltpu.CompilerParams(vmem_limit_bytes=VMEM_LIMIT),
        cost_estimate=project_cost(rows, depth, width),
        name="project_keep",
    )(lengths, decode_host, scaled, weight)


def pack_blocks(first, kv, pick_ref, meta_ref, outs):
    width = kv.shape[1]
    for base in range(0, len(outs), GROUP):
        part = outs[base : base + GROUP]
        top = (first + base) * MAXLEN
        picks = pick_ref[top : top + len(part) * MAXLEN, :]
        blocks = jnp.dot(picks, kv, preferred_element_type=jnp.float32).astype(jnp.bfloat16)
        for i, out in enumerate(part):
            for g in range(width // HD):
                out[g * MAXLEN : (g + 1) * MAXLEN, :] = blocks[
                    i * MAXLEN : (i + 1) * MAXLEN, g * HD : (g + 1) * HD
                ]
            out[width // HD * MAXLEN :, :] = meta_ref[first + base + i].astype(jnp.bfloat16)


def pack_kernel(keep_ref, recv_ref, send_ref, pick_ref, meta_ref, *outs):
    width = keep_ref.shape[1]
    squares = jnp.sum(recv_ref[:, width:] + send_ref[:, width:], axis=1, keepdims=True)
    inverse = lax.rsqrt(squares / D + 1e-05)
    kv = ((keep_ref[...] + recv_ref[:, :width]) * inverse).astype(jnp.bfloat16)
    pack_blocks(0, kv, pick_ref, meta_ref, outs)


def pack(keep, recv, send, picks, metas, order):
    rows, width = keep.shape
    block = jax.ShapeDtypeStruct((width // HD * MAXLEN + META, HD), jnp.bfloat16)
    blocks = pl.pallas_call(
        pack_kernel,
        out_shape=[block] * len(order),
        in_specs=[VMEM] * 5,
        out_specs=[VMEM] * len(order),
        compiler_params=pltpu.CompilerParams(vmem_limit_bytes=VMEM_LIMIT),
        name="pack",
    )(keep, recv, send, picks, metas)
    return dict(zip(order, blocks))


def attend_blocks(blocks, table_ref, q_ref, score_ref, value_ref, acc_ref):
    groups = q_ref.shape[0] // QPK
    scale = HD ** (-0.5)
    flat = QPK * BMAX
    lane = lax.broadcasted_iota(jnp.int32, (flat, MAXLEN), 1)
    beam = lax.broadcasted_iota(jnp.int32, (QPK, BMAX, HD), 1)
    place = lax.broadcasted_iota(jnp.int32, table_ref.shape, 0).astype(jnp.float32)
    work = []
    for block in blocks:
        meta = block[2 * groups * MAXLEN :, :].astype(jnp.float32)
        length = meta[:1, 1:2].astype(jnp.int32)
        entry = jnp.sum(jnp.where(place == meta[:1, :1], table_ref[...], 0.0), axis=0, keepdims=True)
        start = entry[0, 0].astype(jnp.int32)
        count = entry[:1, 1:2].astype(jnp.int32)
        for g in range(groups):
            work.append((block, g, length, pl.ds(start, BMAX), count))
    scores = []
    for block, g, length, at, count in work:
        q = q_ref[g * QPK : (g + 1) * QPK, at, :].reshape(flat, HD).astype(jnp.bfloat16)
        keys = block[2 * g * MAXLEN : (2 * g + 1) * MAXLEN, :]
        raw = lax.dot_general(q, keys, (((1,), (1,)), ((), ())), preferred_element_type=jnp.float32)
        scores.append(jnp.where(lane < length, raw * scale, -jnp.inf))
    tops, owns = [], []
    for (block, g, length, at, count), score in zip(work, scores):
        own = score_ref[g * QPK : (g + 1) * QPK, at, :].reshape(flat, HD)[:, :1]
        owns.append(own)
        tops.append(jnp.maximum(jnp.max(score, axis=1, keepdims=True), own))
    expos = [jnp.exp(score - top) for score, top in zip(scores, tops)]
    own_expos = [jnp.exp(own - top) for own, top in zip(owns, tops)]
    totals = [jnp.sum(e, axis=1, keepdims=True) + o for e, o in zip(expos, own_expos)]
    weights = [(e / t).astype(jnp.bfloat16) for e, t in zip(expos, totals)]
    own_weights = [(o / t).astype(jnp.bfloat16).astype(jnp.float32) for o, t in zip(own_expos, totals)]
    mixes = []
    for (block, g, length, at, count), weight in zip(work, weights):
        values = block[(2 * g + 1) * MAXLEN : (2 * g + 2) * MAXLEN, :]
        mixes.append(jnp.dot(weight, values, preferred_element_type=jnp.float32))
    for (block, g, length, at, count), mix, own in zip(work, mixes, own_weights):
        own = own.reshape(QPK, BMAX, 1) * value_ref[g, at, :][None]
        heads = slice(g * QPK, (g + 1) * QPK)
        acc_ref[heads, at, :] = jnp.where(
            beam < count, mix.reshape(QPK, BMAX, HD) + own, acc_ref[heads, at, :]
        )


def first_kernel(query_ref, own_ref, count_ref, block_ref, q_ref, score_ref, value_ref, table_ref, acc_ref):
    beams = query_ref.shape[0]
    heads = query_ref.shape[1] // HD
    scale = HD ** (-0.5)
    tail = jnp.zeros((BMAX, HD), jnp.float32)
    for g in range(heads // QPK):
        key = own_ref[:, 2 * g * HD : (2 * g + 1) * HD].astype(jnp.float32)
        value_ref[g, :beams, :] = own_ref[:, (2 * g + 1) * HD : (2 * g + 2) * HD].astype(jnp.float32)
        value_ref[g, beams:, :] = tail
        for h in range(g * QPK, (g + 1) * QPK):
            q = query_ref[:, h * HD : (h + 1) * HD].astype(jnp.float32)
            q_ref[h, :beams, :] = q
            q_ref[h, beams:, :] = tail
            score = jnp.sum(q * key, axis=1, keepdims=True) * scale
            score_ref[h, :beams, :] = jnp.broadcast_to(score, (beams, HD))
            score_ref[h, beams:, :] = tail
    lane = lax.broadcasted_iota(jnp.int32, (1, HD), 1)
    start = 0
    for i in range(count_ref.shape[1]):
        count = count_ref[0, i]
        row = jnp.where(lane == 0, start, jnp.where(lane == 1, count, 0))
        table_ref[i : i + 1, :] = row.astype(jnp.float32)
        start = start + count
    acc_ref[...] = jnp.zeros_like(acc_ref)
    attend_blocks([block_ref], table_ref, q_ref, score_ref, value_ref, acc_ref)


def attend_first(query, own, counts, block):
    beams, width = query.shape
    heads = width // HD
    tall = jax.ShapeDtypeStruct((heads, beams + BMAX, HD), jnp.float32)
    return pl.pallas_call(
        first_kernel,
        out_shape=(
            tall,
            tall,
            jax.ShapeDtypeStruct((heads // QPK, beams + BMAX, HD), jnp.float32),
            jax.ShapeDtypeStruct((counts.shape[1], HD), jnp.float32),
            tall,
        ),
        in_specs=[VMEM, VMEM, SMEM, VMEM],
        out_specs=(VMEM,) * 5,
        compiler_params=pltpu.CompilerParams(vmem_limit_bytes=VMEM_LIMIT),
        cost_estimate=pl.CostEstimate(flops=1 << 24, bytes_accessed=4 << 20, transcendentals=0),
        name="attend_first",
    )(query, own, counts, block)


def later_kernel(table_ref, q_ref, score_ref, value_ref, acc_in, *refs, n_blocks, last):
    blocks, rest = refs[:n_blocks], refs[n_blocks:]
    acc_ref = rest[0]
    for base in range(0, n_blocks, GROUP // 2):
        attend_blocks(blocks[base : base + GROUP // 2], table_ref, q_ref, score_ref, value_ref, acc_ref)
    if last:
        out_ref = rest[1]
        beams = out_ref.shape[0]
        for h in range(acc_ref.shape[0]):
            out_ref[:, h * HD : (h + 1) * HD] = acc_ref[h, :beams, :].astype(jnp.bfloat16)


def attend_later(table, q, score, value, acc, blocks, out_shape):
    last = out_shape is not None
    shapes = [jax.ShapeDtypeStruct(acc.shape, acc.dtype)]
    if last:
        shapes.append(out_shape)
    return pl.pallas_call(
        functools.partial(later_kernel, n_blocks=len(blocks), last=last),
        out_shape=shapes,
        in_specs=[VMEM] * (5 + len(blocks)),
        out_specs=[VMEM] * len(shapes),
        input_output_aliases={4: 0},
        compiler_params=pltpu.CompilerParams(vmem_limit_bytes=VMEM_LIMIT),
        cost_estimate=pl.CostEstimate(flops=1 << 24, bytes_accessed=4 << 20, transcendentals=0),
        name="attend_last" if last else "attend_more",
    )(table, q, score, value, acc, *blocks)


def per_device(tokens, norm_gain, kv_weight, lengths, decode_host, beam_counts, beam_query, beam_newkv):
    sections = lax.axis_size("section")
    gain = pltpu.with_memory_space_constraint(norm_gain.reshape(-1, HD), pltpu.HBM)
    tokens = pltpu.with_memory_space_constraint(tokens, pltpu.HBM)
    send, scaled = project_send(tokens, gain, kv_weight)
    recv = lax.ppermute(send, "tensor", [(0, 1), (1, 0)])
    turns = tuple(range(sections - 1, -1, -1))
    keep, picks, metas = project_keep(lengths, decode_host, scaled, kv_weight, turns)
    blocks = pack(keep, recv, send, picks, metas, turns)
    got = {}
    for k in range(1, sections):
        got[k] = lax.ppermute(blocks[k], "section", [(s, s ^ k) for s in range(sections)])
    q, score, value, table, acc = attend_first(beam_query, beam_newkv, beam_counts, blocks[0])
    order = ORDER if sections == len(ORDER) + 1 else tuple(range(sections - 1, 0, -1))
    for part in (order[:4], order[4:-1]):
        (acc,) = attend_later(table, q, score, value, acc, [got[k] for k in part], None)
    late = [got[order[-1]]]
    out_shape = jax.ShapeDtypeStruct(beam_query.shape, jnp.bfloat16)
    return attend_later(table, q, score, value, acc, late, out_shape)[1]


def solution(mesh):
    rows = ("groups", "section")
    placed = (
        P(rows, "tensor"),
        P("tensor"),
        P("tensor", None),
        P(rows, None),
        P(rows, None),
        P(rows, None),
        P(rows, "tensor"),
        P(rows, "tensor"),
    )
    return jax.shard_map(
        per_device,
        mesh=mesh,
        in_specs=placed,
        out_specs=P(rows, "tensor"),
        check_vma=False,
    )
```

```python
import functools

import jax
import jax.numpy as jnp
from jax import lax
from jax.experimental import pallas as pl
from jax.experimental.pallas import tpu as pltpu
from jax.sharding import PartitionSpec as P

D = 8192
QPK = 8
HD = 128
BMAX = 16
MAXLEN = 96
META = 8
STEP = 512
GROUP = 8
FRONT = 2
ORDER = (4, 2, 5, 3, 7, 1, 6)
VMEM_LIMIT = 44 * 1024 * 1024
PROJECT_LIMIT = VMEM_LIMIT

VMEM = pl.BlockSpec(memory_space=pltpu.VMEM)
SMEM = pl.BlockSpec(memory_space=pltpu.SMEM)
HBM = pl.BlockSpec(memory_space=pltpu.HBM)


def weight_copy(w_ref, w_buf, sem, half, c):
    width = w_buf.shape[2]
    columns = pl.ds(pl.multiple_of(half * width, width), width)
    rows = pl.ds(pl.multiple_of(c * STEP, STEP), STEP)
    return pltpu.make_async_copy(w_ref.at[rows, columns], w_buf.at[c], sem.at[c])


def project_send_kernel(tok_ref, gain_hbm, w_ref, out_ref, scaled_ref, gain_buf, gain_ref, tok_buf, w_buf, gain_sem, tok_sem, w_sem):
    half = 1 - lax.axis_index("tensor")
    steps = w_buf.shape[0]
    width = w_buf.shape[2]
    blocks = STEP // HD

    def token_copy(c):
        columns = pl.ds(pl.multiple_of(c * STEP, STEP), STEP)
        return pltpu.make_async_copy(tok_ref.at[:, columns], tok_buf.at[c], tok_sem.at[c])

    def begin(c, _):
        token_copy(c).start()
        weight_copy(w_ref, w_buf, w_sem, half, c).start()
        return _

    def step(c, _):
        token_copy(c).wait()
        squares = out_ref[:, width:]
        for b in range(blocks):
            tok = tok_buf[c, :, b * HD : (b + 1) * HD].astype(jnp.float32)
            scale = gain_ref[pl.ds(c * blocks + b, 1), :]
            scaled_ref[c, :, b * HD : (b + 1) * HD] = (tok * scale).astype(jnp.bfloat16)
            squares = squares + tok * tok
        out_ref[:, width:] = squares
        weight_copy(w_ref, w_buf, w_sem, half, c).wait()
        out_ref[:, :width] += jnp.dot(scaled_ref[c], w_buf[c], preferred_element_type=jnp.float32)
        return _

    gain_copy = pltpu.make_async_copy(gain_hbm, gain_buf, gain_sem.at[0])
    gain_copy.start()
    out_ref[...] = jnp.zeros_like(out_ref)
    lax.fori_loop(0, steps, begin, 0)
    gain_copy.wait()
    gain_ref[...] = gain_buf[...].astype(jnp.float32)
    lax.fori_loop(0, steps, step, 0, unroll=4)


def make_picks(order, me, rows, len_ref, host_ref, pick_ref, meta_ref, slot_ref, start_ref):
    start = 0
    for i in range(len_ref.shape[1]):
        turn = host_ref[0, i] ^ me
        slot_ref[turn] = i
        start_ref[turn] = start
        start = start + len_ref[0, i]
    lane = lax.broadcasted_iota(jnp.int32, (META, HD), 1)
    row_at = lax.broadcasted_iota(jnp.int32, (MAXLEN, rows), 1)
    row_at = row_at - lax.broadcasted_iota(jnp.int32, (MAXLEN, rows), 0)
    for i, k in enumerate(order):
        hit = (row_at == start_ref[k]).astype(jnp.float32).astype(jnp.bfloat16)
        pick_ref[i * MAXLEN : (i + 1) * MAXLEN, :] = hit
        slot = slot_ref[k]
        meta = jnp.where(lane == 0, slot, jnp.where(lane == 1, len_ref[0, slot], 0))
        meta_ref[i] = meta.astype(jnp.float32)


def project_keep_kernel(len_hbm, host_hbm, scaled_ref, w_ref, out_ref, pick_ref, meta_ref, w_buf, w_sem, len_ref, host_ref, small_sem, slot_ref, start_ref, *, order):
    half = lax.axis_index("tensor")
    steps = w_buf.shape[0]
    len_copy = pltpu.make_async_copy(len_hbm, len_ref, small_sem.at[0])
    host_copy = pltpu.make_async_copy(host_hbm, host_ref, small_sem.at[1])
    len_copy.start()
    host_copy.start()
    for c in range(steps):
        weight_copy(w_ref, w_buf, w_sem, half, c).start()
    len_copy.wait()
    host_copy.wait()
    make_picks(order, lax.axis_index("section"), out_ref.shape[0], len_ref, host_ref, pick_ref, meta_ref, slot_ref, start_ref)
    for c in range(steps):
        weight_copy(w_ref, w_buf, w_sem, half, c).wait()
        part = jnp.dot(scaled_ref[c], w_buf[c], preferred_element_type=jnp.float32)
        if c == 0:
            out_ref[...] = part
        else:
            out_ref[...] += part


def project_cost(rows, depth, width):
    return pl.CostEstimate(
        flops=2 * rows * depth * width,
        bytes_accessed=2 * depth * (rows + width) + 4 * rows * width,
        transcendentals=0,
    )


def project_send(tokens, gain, weight):
    rows, depth = tokens.shape
    width = weight.shape[1] // 2
    steps = depth // STEP
    return pl.pallas_call(
        project_send_kernel,
        out_shape=(
            jax.ShapeDtypeStruct((rows, width + HD), jnp.float32),
            jax.ShapeDtypeStruct((steps, rows, STEP), jnp.bfloat16),
        ),
        in_specs=[HBM, HBM, HBM],
        out_specs=(VMEM, VMEM),
        scratch_shapes=[
            pltpu.VMEM(gain.shape, jnp.bfloat16),
            pltpu.VMEM(gain.shape, jnp.float32),
            pltpu.VMEM((steps, rows, STEP), jnp.bfloat16),
            pltpu.VMEM((steps, STEP, width), jnp.bfloat16),
            pltpu.SemaphoreType.DMA((1,)),
            pltpu.SemaphoreType.DMA((steps,)),
            pltpu.SemaphoreType.DMA((steps,)),
        ],
        compiler_params=pltpu.CompilerParams(vmem_limit_bytes=PROJECT_LIMIT),
        cost_estimate=project_cost(rows, depth, width),
        name="project_send",
    )(tokens, gain, weight)


def project_keep(lengths, decode_host, scaled, weight, order):
    steps, rows, _ = scaled.shape
    depth = steps * STEP
    width = weight.shape[1] // 2
    sections = len(order)
    return pl.pallas_call(
        functools.partial(project_keep_kernel, order=order),
        out_shape=(
            jax.ShapeDtypeStruct((rows, width), jnp.float32),
            jax.ShapeDtypeStruct((sections * MAXLEN, rows), jnp.bfloat16),
            jax.ShapeDtypeStruct((sections, META, HD), jnp.float32),
        ),
        in_specs=[HBM, HBM, VMEM, HBM],
        out_specs=(VMEM, VMEM, VMEM),
        scratch_shapes=[
            pltpu.VMEM((steps, STEP, width), jnp.bfloat16),
            pltpu.SemaphoreType.DMA((steps,)),
            pltpu.SMEM((1, sections), jnp.int32),
            pltpu.SMEM((1, sections), jnp.int32),
            pltpu.SemaphoreType.DMA((2,)),
            pltpu.SMEM((sections,), jnp.int32),
            pltpu.SMEM((sections,), jnp.int32),
        ],
        compiler_params=pltpu.CompilerParams(vmem_limit_bytes=VMEM_LIMIT),
        cost_estimate=project_cost(rows, depth, width),
        name="project_keep",
    )(lengths, decode_host, scaled, weight)


def pack_blocks(first, kv, pick_ref, meta_ref, outs):
    width = kv.shape[1]
    for base in range(0, len(outs), GROUP):
        part = outs[base : base + GROUP]
        top = (first + base) * MAXLEN
        picks = pick_ref[top : top + len(part) * MAXLEN, :]
        blocks = jnp.dot(picks, kv, preferred_element_type=jnp.float32).astype(jnp.bfloat16)
        for i, out in enumerate(part):
            for g in range(width // HD):
                out[g * MAXLEN : (g + 1) * MAXLEN, :] = blocks[
                    i * MAXLEN : (i + 1) * MAXLEN, g * HD : (g + 1) * HD
                ]
            out[width // HD * MAXLEN :, :] = meta_ref[first + base + i].astype(jnp.bfloat16)


def pack_kernel(keep_ref, recv_ref, send_ref, pick_ref, meta_ref, *outs):
    width = keep_ref.shape[1]
    squares = jnp.sum(recv_ref[:, width:] + send_ref[:, width:], axis=1, keepdims=True)
    inverse = lax.rsqrt(squares / D + 1e-05)
    kv = ((keep_ref[...] + recv_ref[:, :width]) * inverse).astype(jnp.bfloat16)
    pack_blocks(0, kv, pick_ref, meta_ref, outs)


def pack(keep, recv, send, picks, metas, order):
    rows, width = keep.shape
    block = jax.ShapeDtypeStruct((width // HD * MAXLEN + META, HD), jnp.bfloat16)
    blocks = pl.pallas_call(
        pack_kernel,
        out_shape=[block] * len(order),
        in_specs=[VMEM] * 5,
        out_specs=[VMEM] * len(order),
        compiler_params=pltpu.CompilerParams(vmem_limit_bytes=VMEM_LIMIT),
        name="pack",
    )(keep, recv, send, picks, metas)
    return dict(zip(order, blocks))


def attend_blocks(blocks, table_ref, q_ref, score_ref, value_ref, acc_ref):
    groups = q_ref.shape[0] // QPK
    scale = HD ** (-0.5)
    flat = QPK * BMAX
    lane = lax.broadcasted_iota(jnp.int32, (flat, MAXLEN), 1)
    beam = lax.broadcasted_iota(jnp.int32, (QPK, BMAX, HD), 1)
    place = lax.broadcasted_iota(jnp.int32, table_ref.shape, 0).astype(jnp.float32)
    work = []
    for block in blocks:
        meta = block[2 * groups * MAXLEN :, :].astype(jnp.float32)
        length = meta[:1, 1:2].astype(jnp.int32)
        entry = jnp.sum(jnp.where(place == meta[:1, :1], table_ref[...], 0.0), axis=0, keepdims=True)
        start = entry[0, 0].astype(jnp.int32)
        count = entry[:1, 1:2].astype(jnp.int32)
        for g in range(groups):
            work.append((block, g, length, pl.ds(start, BMAX), count))
    scores = []
    for block, g, length, at, count in work:
        q = q_ref[g * QPK : (g + 1) * QPK, at, :].reshape(flat, HD).astype(jnp.bfloat16)
        keys = block[2 * g * MAXLEN : (2 * g + 1) * MAXLEN, :]
        raw = lax.dot_general(q, keys, (((1,), (1,)), ((), ())), preferred_element_type=jnp.float32)
        scores.append(jnp.where(lane < length, raw * scale, -jnp.inf))
    tops, owns = [], []
    for (block, g, length, at, count), score in zip(work, scores):
        own = score_ref[g * QPK : (g + 1) * QPK, at, :].reshape(flat, HD)[:, :1]
        owns.append(own)
        tops.append(jnp.maximum(jnp.max(score, axis=1, keepdims=True), own))
    expos = [jnp.exp(score - top) for score, top in zip(scores, tops)]
    own_expos = [jnp.exp(own - top) for own, top in zip(owns, tops)]
    totals = [jnp.sum(e, axis=1, keepdims=True) + o for e, o in zip(expos, own_expos)]
    weights = [(e / t).astype(jnp.bfloat16) for e, t in zip(expos, totals)]
    own_weights = [(o / t).astype(jnp.bfloat16).astype(jnp.float32) for o, t in zip(own_expos, totals)]
    mixes = []
    for (block, g, length, at, count), weight in zip(work, weights):
        values = block[(2 * g + 1) * MAXLEN : (2 * g + 2) * MAXLEN, :]
        mixes.append(jnp.dot(weight, values, preferred_element_type=jnp.float32))
    for (block, g, length, at, count), mix, own in zip(work, mixes, own_weights):
        own = own.reshape(QPK, BMAX, 1) * value_ref[g, at, :][None]
        heads = slice(g * QPK, (g + 1) * QPK)
        acc_ref[heads, at, :] = jnp.where(
            beam < count, mix.reshape(QPK, BMAX, HD) + own, acc_ref[heads, at, :]
        )


def first_kernel(query_ref, own_ref, count_ref, block_ref, q_ref, score_ref, value_ref, table_ref, acc_ref):
    beams = query_ref.shape[0]
    heads = query_ref.shape[1] // HD
    scale = HD ** (-0.5)
    tail = jnp.zeros((BMAX, HD), jnp.float32)
    for g in range(heads // QPK):
        key = own_ref[:, 2 * g * HD : (2 * g + 1) * HD].astype(jnp.float32)
        value_ref[g, :beams, :] = own_ref[:, (2 * g + 1) * HD : (2 * g + 2) * HD].astype(jnp.float32)
        value_ref[g, beams:, :] = tail
        for h in range(g * QPK, (g + 1) * QPK):
            q = query_ref[:, h * HD : (h + 1) * HD].astype(jnp.float32)
            q_ref[h, :beams, :] = q
            q_ref[h, beams:, :] = tail
            score = jnp.sum(q * key, axis=1, keepdims=True) * scale
            score_ref[h, :beams, :] = jnp.broadcast_to(score, (beams, HD))
            score_ref[h, beams:, :] = tail
    lane = lax.broadcasted_iota(jnp.int32, (1, HD), 1)
    start = 0
    for i in range(count_ref.shape[1]):
        count = count_ref[0, i]
        row = jnp.where(lane == 0, start, jnp.where(lane == 1, count, 0))
        table_ref[i : i + 1, :] = row.astype(jnp.float32)
        start = start + count
    acc_ref[...] = jnp.zeros_like(acc_ref)
    attend_blocks([block_ref], table_ref, q_ref, score_ref, value_ref, acc_ref)


def attend_first(query, own, counts, block):
    beams, width = query.shape
    heads = width // HD
    tall = jax.ShapeDtypeStruct((heads, beams + BMAX, HD), jnp.float32)
    return pl.pallas_call(
        first_kernel,
        out_shape=(
            tall,
            tall,
            jax.ShapeDtypeStruct((heads // QPK, beams + BMAX, HD), jnp.float32),
            jax.ShapeDtypeStruct((counts.shape[1], HD), jnp.float32),
            tall,
        ),
        in_specs=[VMEM, VMEM, SMEM, VMEM],
        out_specs=(VMEM,) * 5,
        compiler_params=pltpu.CompilerParams(vmem_limit_bytes=VMEM_LIMIT),
        cost_estimate=pl.CostEstimate(flops=1 << 24, bytes_accessed=4 << 20, transcendentals=0),
        name="attend_first",
    )(query, own, counts, block)


def later_kernel(table_ref, q_ref, score_ref, value_ref, acc_in, *refs, n_blocks, last):
    blocks, rest = refs[:n_blocks], refs[n_blocks:]
    acc_ref = rest[0]
    for base in range(0, n_blocks, GROUP // 2):
        attend_blocks(blocks[base : base + GROUP // 2], table_ref, q_ref, score_ref, value_ref, acc_ref)
    if last:
        out_ref = rest[1]
        beams = out_ref.shape[0]
        for h in range(acc_ref.shape[0]):
            out_ref[:, h * HD : (h + 1) * HD] = acc_ref[h, :beams, :].astype(jnp.bfloat16)


def attend_later(table, q, score, value, acc, blocks, out_shape):
    last = out_shape is not None
    shapes = [jax.ShapeDtypeStruct(acc.shape, acc.dtype)]
    if last:
        shapes.append(out_shape)
    return pl.pallas_call(
        functools.partial(later_kernel, n_blocks=len(blocks), last=last),
        out_shape=shapes,
        in_specs=[VMEM] * (5 + len(blocks)),
        out_specs=[VMEM] * len(shapes),
        input_output_aliases={4: 0},
        compiler_params=pltpu.CompilerParams(vmem_limit_bytes=VMEM_LIMIT),
        cost_estimate=pl.CostEstimate(flops=1 << 24, bytes_accessed=4 << 20, transcendentals=0),
        name="attend_last" if last else "attend_more",
    )(table, q, score, value, acc, *blocks)


def per_device(tokens, norm_gain, kv_weight, lengths, decode_host, beam_counts, beam_query, beam_newkv):
    sections = lax.axis_size("section")
    gain = pltpu.with_memory_space_constraint(norm_gain.reshape(-1, HD), pltpu.HBM)
    tokens = pltpu.with_memory_space_constraint(tokens, pltpu.HBM)
    send, scaled = project_send(tokens, gain, kv_weight)
    recv = lax.ppermute(send, "tensor", [(0, 1), (1, 0)])
    turns = tuple(range(sections - 1, -1, -1))
    keep, picks, metas = project_keep(lengths, decode_host, scaled, kv_weight, turns)
    blocks = pack(keep, recv, send, picks, metas, turns)
    got = {}
    for k in range(1, sections):
        got[k] = lax.ppermute(blocks[k], "section", [(s, s ^ k) for s in range(sections)])
    q, score, value, table, acc = attend_first(beam_query, beam_newkv, beam_counts, blocks[0])
    order = ORDER if sections == len(ORDER) + 1 else tuple(range(sections - 1, 0, -1))
    for part in (order[:4], order[4:-1]):
        (acc,) = attend_later(table, q, score, value, acc, [got[k] for k in part], None)
    late = [got[order[-1]]]
    out_shape = jax.ShapeDtypeStruct(beam_query.shape, jnp.bfloat16)
    return attend_later(table, q, score, value, acc, late, out_shape)[1]


def solution(mesh):
    rows = ("groups", "section")
    placed = (
        P(rows, "tensor"),
        P("tensor"),
        P("tensor", None),
        P(rows, None),
        P(rows, None),
        P(rows, None),
        P(rows, "tensor"),
        P(rows, "tensor"),
    )
    return jax.shard_map(
        per_device,
        mesh=mesh,
        in_specs=placed,
        out_specs=P(rows, "tensor"),
        check_vma=False,
    )
```

```python
import functools

import jax
import jax.numpy as jnp
from jax import lax
from jax.experimental import pallas as pl
from jax.experimental.pallas import tpu as pltpu
from jax.sharding import PartitionSpec as P

D = 8192
QPK = 8
HD = 128
BMAX = 16
MAXLEN = 96
META = 8
STEP = 1024
GROUP = 8
FRONT = 2
ORDER = (4, 2, 5, 3, 7, 1, 6)
VMEM_LIMIT = 44 * 1024 * 1024
PROJECT_LIMIT = VMEM_LIMIT

VMEM = pl.BlockSpec(memory_space=pltpu.VMEM)
SMEM = pl.BlockSpec(memory_space=pltpu.SMEM)
HBM = pl.BlockSpec(memory_space=pltpu.HBM)


def weight_copy(w_ref, w_buf, sem, half, c):
    width = w_buf.shape[2]
    columns = pl.ds(pl.multiple_of(half * width, width), width)
    rows = pl.ds(pl.multiple_of(c * STEP, STEP), STEP)
    return pltpu.make_async_copy(w_ref.at[rows, columns], w_buf.at[c], sem.at[c])


def project_send_kernel(tok_ref, gain_hbm, w_ref, out_ref, scaled_ref, gain_buf, gain_ref, tok_buf, w_buf, gain_sem, tok_sem, w_sem):
    half = 1 - lax.axis_index("tensor")
    steps = w_buf.shape[0]
    width = w_buf.shape[2]
    blocks = STEP // HD

    def token_copy(c):
        columns = pl.ds(pl.multiple_of(c * STEP, STEP), STEP)
        return pltpu.make_async_copy(tok_ref.at[:, columns], tok_buf.at[c], tok_sem.at[c])

    def begin(c, _):
        token_copy(c).start()
        weight_copy(w_ref, w_buf, w_sem, half, c).start()
        return _

    def step(c, _):
        token_copy(c).wait()
        squares = out_ref[:, width:]
        for b in range(blocks):
            tok = tok_buf[c, :, b * HD : (b + 1) * HD].astype(jnp.float32)
            scale = gain_ref[pl.ds(c * blocks + b, 1), :]
            scaled_ref[c, :, b * HD : (b + 1) * HD] = (tok * scale).astype(jnp.bfloat16)
            squares = squares + tok * tok
        out_ref[:, width:] = squares
        weight_copy(w_ref, w_buf, w_sem, half, c).wait()
        out_ref[:, :width] += jnp.dot(scaled_ref[c], w_buf[c], preferred_element_type=jnp.float32)
        return _

    gain_copy = pltpu.make_async_copy(gain_hbm, gain_buf, gain_sem.at[0])
    gain_copy.start()
    out_ref[...] = jnp.zeros_like(out_ref)
    lax.fori_loop(0, steps, begin, 0)
    gain_copy.wait()
    gain_ref[...] = gain_buf[...].astype(jnp.float32)
    lax.fori_loop(0, steps, step, 0, unroll=2)


def make_picks(order, me, rows, len_ref, host_ref, pick_ref, meta_ref, slot_ref, start_ref):
    start = 0
    for i in range(len_ref.shape[1]):
        turn = host_ref[0, i] ^ me
        slot_ref[turn] = i
        start_ref[turn] = start
        start = start + len_ref[0, i]
    lane = lax.broadcasted_iota(jnp.int32, (META, HD), 1)
    row_at = lax.broadcasted_iota(jnp.int32, (MAXLEN, rows), 1)
    row_at = row_at - lax.broadcasted_iota(jnp.int32, (MAXLEN, rows), 0)
    for i, k in enumerate(order):
        hit = (row_at == start_ref[k]).astype(jnp.float32).astype(jnp.bfloat16)
        pick_ref[i * MAXLEN : (i + 1) * MAXLEN, :] = hit
        slot = slot_ref[k]
        meta = jnp.where(lane == 0, slot, jnp.where(lane == 1, len_ref[0, slot], 0))
        meta_ref[i] = meta.astype(jnp.float32)


def project_keep_kernel(len_hbm, host_hbm, scaled_ref, w_ref, out_ref, pick_ref, meta_ref, w_buf, w_sem, len_ref, host_ref, small_sem, slot_ref, start_ref, *, order):
    half = lax.axis_index("tensor")
    steps = w_buf.shape[0]
    len_copy = pltpu.make_async_copy(len_hbm, len_ref, small_sem.at[0])
    host_copy = pltpu.make_async_copy(host_hbm, host_ref, small_sem.at[1])
    len_copy.start()
    host_copy.start()
    for c in range(steps):
        weight_copy(w_ref, w_buf, w_sem, half, c).start()
    len_copy.wait()
    host_copy.wait()
    make_picks(order, lax.axis_index("section"), out_ref.shape[0], len_ref, host_ref, pick_ref, meta_ref, slot_ref, start_ref)
    for c in range(steps):
        weight_copy(w_ref, w_buf, w_sem, half, c).wait()
        part = jnp.dot(scaled_ref[c], w_buf[c], preferred_element_type=jnp.float32)
        if c == 0:
            out_ref[...] = part
        else:
            out_ref[...] += part


def project_cost(rows, depth, width):
    return pl.CostEstimate(
        flops=2 * rows * depth * width,
        bytes_accessed=2 * depth * (rows + width) + 4 * rows * width,
        transcendentals=0,
    )


def project_send(tokens, gain, weight):
    rows, depth = tokens.shape
    width = weight.shape[1] // 2
    steps = depth // STEP
    return pl.pallas_call(
        project_send_kernel,
        out_shape=(
            jax.ShapeDtypeStruct((rows, width + HD), jnp.float32),
            jax.ShapeDtypeStruct((steps, rows, STEP), jnp.bfloat16),
        ),
        in_specs=[HBM, HBM, HBM],
        out_specs=(VMEM, VMEM),
        scratch_shapes=[
            pltpu.VMEM(gain.shape, jnp.bfloat16),
            pltpu.VMEM(gain.shape, jnp.float32),
            pltpu.VMEM((steps, rows, STEP), jnp.bfloat16),
            pltpu.VMEM((steps, STEP, width), jnp.bfloat16),
            pltpu.SemaphoreType.DMA((1,)),
            pltpu.SemaphoreType.DMA((steps,)),
            pltpu.SemaphoreType.DMA((steps,)),
        ],
        compiler_params=pltpu.CompilerParams(vmem_limit_bytes=PROJECT_LIMIT),
        cost_estimate=project_cost(rows, depth, width),
        name="project_send",
    )(tokens, gain, weight)


def project_keep(lengths, decode_host, scaled, weight, order):
    steps, rows, _ = scaled.shape
    depth = steps * STEP
    width = weight.shape[1] // 2
    sections = len(order)
    return pl.pallas_call(
        functools.partial(project_keep_kernel, order=order),
        out_shape=(
            jax.ShapeDtypeStruct((rows, width), jnp.float32),
            jax.ShapeDtypeStruct((sections * MAXLEN, rows), jnp.bfloat16),
            jax.ShapeDtypeStruct((sections, META, HD), jnp.float32),
        ),
        in_specs=[HBM, HBM, VMEM, HBM],
        out_specs=(VMEM, VMEM, VMEM),
        scratch_shapes=[
            pltpu.VMEM((steps, STEP, width), jnp.bfloat16),
            pltpu.SemaphoreType.DMA((steps,)),
            pltpu.SMEM((1, sections), jnp.int32),
            pltpu.SMEM((1, sections), jnp.int32),
            pltpu.SemaphoreType.DMA((2,)),
            pltpu.SMEM((sections,), jnp.int32),
            pltpu.SMEM((sections,), jnp.int32),
        ],
        compiler_params=pltpu.CompilerParams(vmem_limit_bytes=VMEM_LIMIT),
        cost_estimate=project_cost(rows, depth, width),
        name="project_keep",
    )(lengths, decode_host, scaled, weight)


def pack_blocks(first, kv, pick_ref, meta_ref, outs):
    width = kv.shape[1]
    for base in range(0, len(outs), GROUP):
        part = outs[base : base + GROUP]
        top = (first + base) * MAXLEN
        picks = pick_ref[top : top + len(part) * MAXLEN, :]
        blocks = jnp.dot(picks, kv, preferred_element_type=jnp.float32).astype(jnp.bfloat16)
        for i, out in enumerate(part):
            for g in range(width // HD):
                out[g * MAXLEN : (g + 1) * MAXLEN, :] = blocks[
                    i * MAXLEN : (i + 1) * MAXLEN, g * HD : (g + 1) * HD
                ]
            out[width // HD * MAXLEN :, :] = meta_ref[first + base + i].astype(jnp.bfloat16)


def pack_kernel(keep_ref, recv_ref, send_ref, pick_ref, meta_ref, *outs):
    width = keep_ref.shape[1]
    squares = jnp.sum(recv_ref[:, width:] + send_ref[:, width:], axis=1, keepdims=True)
    inverse = lax.rsqrt(squares / D + 1e-05)
    kv = ((keep_ref[...] + recv_ref[:, :width]) * inverse).astype(jnp.bfloat16)
    pack_blocks(0, kv, pick_ref, meta_ref, outs)


def pack(keep, recv, send, picks, metas, order):
    rows, width = keep.shape
    block = jax.ShapeDtypeStruct((width // HD * MAXLEN + META, HD), jnp.bfloat16)
    blocks = pl.pallas_call(
        pack_kernel,
        out_shape=[block] * len(order),
        in_specs=[VMEM] * 5,
        out_specs=[VMEM] * len(order),
        compiler_params=pltpu.CompilerParams(vmem_limit_bytes=VMEM_LIMIT),
        name="pack",
    )(keep, recv, send, picks, metas)
    return dict(zip(order, blocks))


def attend_blocks(blocks, table_ref, q_ref, score_ref, value_ref, acc_ref):
    groups = q_ref.shape[0] // QPK
    scale = HD ** (-0.5)
    flat = QPK * BMAX
    lane = lax.broadcasted_iota(jnp.int32, (flat, MAXLEN), 1)
    beam = lax.broadcasted_iota(jnp.int32, (QPK, BMAX, HD), 1)
    place = lax.broadcasted_iota(jnp.int32, table_ref.shape, 0).astype(jnp.float32)
    work = []
    for block in blocks:
        meta = block[2 * groups * MAXLEN :, :].astype(jnp.float32)
        length = meta[:1, 1:2].astype(jnp.int32)
        entry = jnp.sum(jnp.where(place == meta[:1, :1], table_ref[...], 0.0), axis=0, keepdims=True)
        start = entry[0, 0].astype(jnp.int32)
        count = entry[:1, 1:2].astype(jnp.int32)
        for g in range(groups):
            work.append((block, g, length, pl.ds(start, BMAX), count))
    scores = []
    for block, g, length, at, count in work:
        q = q_ref[g * QPK : (g + 1) * QPK, at, :].reshape(flat, HD).astype(jnp.bfloat16)
        keys = block[2 * g * MAXLEN : (2 * g + 1) * MAXLEN, :]
        raw = lax.dot_general(q, keys, (((1,), (1,)), ((), ())), preferred_element_type=jnp.float32)
        scores.append(jnp.where(lane < length, raw * scale, -jnp.inf))
    tops, owns = [], []
    for (block, g, length, at, count), score in zip(work, scores):
        own = score_ref[g * QPK : (g + 1) * QPK, at, :].reshape(flat, HD)[:, :1]
        owns.append(own)
        tops.append(jnp.maximum(jnp.max(score, axis=1, keepdims=True), own))
    expos = [jnp.exp(score - top) for score, top in zip(scores, tops)]
    own_expos = [jnp.exp(own - top) for own, top in zip(owns, tops)]
    totals = [jnp.sum(e, axis=1, keepdims=True) + o for e, o in zip(expos, own_expos)]
    weights = [(e / t).astype(jnp.bfloat16) for e, t in zip(expos, totals)]
    own_weights = [(o / t).astype(jnp.bfloat16).astype(jnp.float32) for o, t in zip(own_expos, totals)]
    mixes = []
    for (block, g, length, at, count), weight in zip(work, weights):
        values = block[(2 * g + 1) * MAXLEN : (2 * g + 2) * MAXLEN, :]
        mixes.append(jnp.dot(weight, values, preferred_element_type=jnp.float32))
    for (block, g, length, at, count), mix, own in zip(work, mixes, own_weights):
        own = own.reshape(QPK, BMAX, 1) * value_ref[g, at, :][None]
        heads = slice(g * QPK, (g + 1) * QPK)
        acc_ref[heads, at, :] = jnp.where(
            beam < count, mix.reshape(QPK, BMAX, HD) + own, acc_ref[heads, at, :]
        )


def first_kernel(query_ref, own_ref, count_ref, block_ref, q_ref, score_ref, value_ref, table_ref, acc_ref):
    beams = query_ref.shape[0]
    heads = query_ref.shape[1] // HD
    scale = HD ** (-0.5)
    tail = jnp.zeros((BMAX, HD), jnp.float32)
    for g in range(heads // QPK):
        key = own_ref[:, 2 * g * HD : (2 * g + 1) * HD].astype(jnp.float32)
        value_ref[g, :beams, :] = own_ref[:, (2 * g + 1) * HD : (2 * g + 2) * HD].astype(jnp.float32)
        value_ref[g, beams:, :] = tail
        for h in range(g * QPK, (g + 1) * QPK):
            q = query_ref[:, h * HD : (h + 1) * HD].astype(jnp.float32)
            q_ref[h, :beams, :] = q
            q_ref[h, beams:, :] = tail
            score = jnp.sum(q * key, axis=1, keepdims=True) * scale
            score_ref[h, :beams, :] = jnp.broadcast_to(score, (beams, HD))
            score_ref[h, beams:, :] = tail
    lane = lax.broadcasted_iota(jnp.int32, (1, HD), 1)
    start = 0
    for i in range(count_ref.shape[1]):
        count = count_ref[0, i]
        row = jnp.where(lane == 0, start, jnp.where(lane == 1, count, 0))
        table_ref[i : i + 1, :] = row.astype(jnp.float32)
        start = start + count
    acc_ref[...] = jnp.zeros_like(acc_ref)
    attend_blocks([block_ref], table_ref, q_ref, score_ref, value_ref, acc_ref)


def attend_first(query, own, counts, block):
    beams, width = query.shape
    heads = width // HD
    tall = jax.ShapeDtypeStruct((heads, beams + BMAX, HD), jnp.float32)
    return pl.pallas_call(
        first_kernel,
        out_shape=(
            tall,
            tall,
            jax.ShapeDtypeStruct((heads // QPK, beams + BMAX, HD), jnp.float32),
            jax.ShapeDtypeStruct((counts.shape[1], HD), jnp.float32),
            tall,
        ),
        in_specs=[VMEM, VMEM, SMEM, VMEM],
        out_specs=(VMEM,) * 5,
        compiler_params=pltpu.CompilerParams(vmem_limit_bytes=VMEM_LIMIT),
        cost_estimate=pl.CostEstimate(flops=1 << 24, bytes_accessed=4 << 20, transcendentals=0),
        name="attend_first",
    )(query, own, counts, block)


def later_kernel(table_ref, q_ref, score_ref, value_ref, acc_in, *refs, n_blocks, last):
    blocks, rest = refs[:n_blocks], refs[n_blocks:]
    acc_ref = rest[0]
    for base in range(0, n_blocks, GROUP // 2):
        attend_blocks(blocks[base : base + GROUP // 2], table_ref, q_ref, score_ref, value_ref, acc_ref)
    if last:
        out_ref = rest[1]
        beams = out_ref.shape[0]
        for h in range(acc_ref.shape[0]):
            out_ref[:, h * HD : (h + 1) * HD] = acc_ref[h, :beams, :].astype(jnp.bfloat16)


def attend_later(table, q, score, value, acc, blocks, out_shape):
    last = out_shape is not None
    shapes = [jax.ShapeDtypeStruct(acc.shape, acc.dtype)]
    if last:
        shapes.append(out_shape)
    return pl.pallas_call(
        functools.partial(later_kernel, n_blocks=len(blocks), last=last),
        out_shape=shapes,
        in_specs=[VMEM] * (5 + len(blocks)),
        out_specs=[VMEM] * len(shapes),
        input_output_aliases={4: 0},
        compiler_params=pltpu.CompilerParams(vmem_limit_bytes=VMEM_LIMIT),
        cost_estimate=pl.CostEstimate(flops=1 << 24, bytes_accessed=4 << 20, transcendentals=0),
        name="attend_last" if last else "attend_more",
    )(table, q, score, value, acc, *blocks)


def per_device(tokens, norm_gain, kv_weight, lengths, decode_host, beam_counts, beam_query, beam_newkv):
    sections = lax.axis_size("section")
    gain = pltpu.with_memory_space_constraint(norm_gain.reshape(-1, HD), pltpu.HBM)
    tokens = pltpu.with_memory_space_constraint(tokens, pltpu.HBM)
    send, scaled = project_send(tokens, gain, kv_weight)
    recv = lax.ppermute(send, "tensor", [(0, 1), (1, 0)])
    turns = tuple(range(sections - 1, -1, -1))
    keep, picks, metas = project_keep(lengths, decode_host, scaled, kv_weight, turns)
    blocks = pack(keep, recv, send, picks, metas, turns)
    got = {}
    for k in range(1, sections):
        got[k] = lax.ppermute(blocks[k], "section", [(s, s ^ k) for s in range(sections)])
    q, score, value, table, acc = attend_first(beam_query, beam_newkv, beam_counts, blocks[0])
    order = ORDER if sections == len(ORDER) + 1 else tuple(range(sections - 1, 0, -1))
    for part in (order[:4], order[4:-1]):
        (acc,) = attend_later(table, q, score, value, acc, [got[k] for k in part], None)
    late = [got[order[-1]]]
    out_shape = jax.ShapeDtypeStruct(beam_query.shape, jnp.bfloat16)
    return attend_later(table, q, score, value, acc, late, out_shape)[1]


def solution(mesh):
    rows = ("groups", "section")
    placed = (
        P(rows, "tensor"),
        P("tensor"),
        P("tensor", None),
        P(rows, None),
        P(rows, None),
        P(rows, None),
        P(rows, "tensor"),
        P(rows, "tensor"),
    )
    return jax.shard_map(
        per_device,
        mesh=mesh,
        in_specs=placed,
        out_specs=P(rows, "tensor"),
        check_vma=False,
    )
```
